256 devices in a mesh: tm: 2 (over x_lo), sx: 32 (over z, x_hi, core), sy: 4 (over y).
Axes of the slice: x: 4 (x_hi: 2, x_lo: 2; x = x_hi * 2 + x_lo), y: 4, z: 8, core: 2. Of those that a mesh axis runs over, the one named last changes fastest.
Arguments:
- forcing: float32 [8, 256, 64, 16, 128], P('tm', 'sx', 'sy'), may hold values from -6 to 6
- initial: float32 [8, 256, 64, 16, 128], P('tm', 'sx', 'sy'), may hold values from -3 to 3
- conductance: float32 [8, 256, 64, 16], P('tm', 'sx', 'sy'), may hold values from 0.5 to 1.5
- counts: int32 [32, 4], P('sx', 'sy'), may hold values from 1024 to 2048, as said below
- block_matrix: float32 [128, 128], replicated, may hold values from -1.1 to 11.1
- precond: float32 [128, 128], replicated, may hold values from -0.011 to 0.111
- face_coupling: float32 [6, 128, 128], replicated, may hold values from -1 to 1
- time_coupling: float32 [64, 128], replicated, may hold values from -3 to 23
Outputs:
- adjoint: float32 [8, 256, 64, 16, 128], P('tm', 'sx', 'sy')
The draws below stay inside these ranges and needn't reach their ends.
Inputs may be any that keep to these rules, and one draw needn't show every extreme that they name: `counts`: active elements of a tile are those whose position in the order x, y, z (z fastest) is below the tile's count; some tile has all 2048 active.
All inputs are finite; a program needn't handle non-finite values.
Results may differ from the reference program's by a relative error of at most 0.00012.
Values sent between devices are 32-bit elements; how exact they have to be, the bound alone decides.
No kernel may reach another device: no remote copies, remote signals or barrier semaphores. Data moves between devices by JAX's collectives and lax.ppermute only.
A program may use at most 128 MiB of HBM per device.

```python
import math
import jax
import jax.numpy as jnp
from jax import lax

EX = 8
EY = 16
EZ = 16
SWEEPS = 2
SPACE = 64
BLOCK = 128
NT = 8
NXE = 256
NYE = 64
ELEMS = 2048


def draw_counts(key, part):
    key = jax.random.fold_in(key, 11)
    tiles_x = NXE // EX
    tiles_y = NYE // EY
    first_key, second_key = jax.random.split(key)
    values = jax.random.randint(first_key, (tiles_x, tiles_y), ELEMS // 2, ELEMS + 1)
    chosen = jax.random.randint(second_key, (), 0, tiles_x * tiles_y)
    flat_idx = jnp.arange(tiles_x * tiles_y, dtype=jnp.int32).reshape(tiles_x, tiles_y)
    return jnp.where(flat_idx == chosen, ELEMS, values).astype(jnp.int32)


def draw_block_matrix(key, part):
    key = jax.random.fold_in(key, 3)
    noise = jnp.clip(jax.random.normal(key, (BLOCK, BLOCK), jnp.float32), -4.0, 4.0)
    return 10.0 * (jnp.eye(BLOCK, dtype=jnp.float32) + 0.3 / math.sqrt(BLOCK) * noise)


def draw_precond(key, part):
    key = jax.random.fold_in(key, 5)
    noise = jnp.clip(jax.random.normal(key, (BLOCK, BLOCK), jnp.float32), -4.0, 4.0)
    ident = jnp.eye(BLOCK, dtype=jnp.float32)
    swapped = jnp.roll(ident, SPACE, axis=1)
    return 0.1 * (ident + 0.5 * swapped + 0.3 / math.sqrt(BLOCK) * noise)


def draw_time_coupling(key, part):
    key = jax.random.fold_in(key, 7)
    noise = jnp.clip(jax.random.normal(key, (SPACE, BLOCK), jnp.float32), -4.0, 4.0)
    ident = jnp.eye(SPACE, BLOCK, k=SPACE, dtype=jnp.float32)
    return 20.0 * (ident + 0.3 / math.sqrt(SPACE) * noise)


def shard_levels(key, extent, shards, smallest, high):
    def one(axis_at, blocks):
        draws = jax.random.uniform(jax.random.fold_in(jax.random.fold_in(key, 6), axis_at), (blocks,), jnp.float32, smallest / len(shards), high / len(shards))
        return jnp.repeat(jnp.exp(draws), extent[axis_at] // blocks).reshape((-1,) + (1,) * (len(extent) - axis_at - 1))

    gain = one(*shards[0])
    for cut in shards[1:]:
        gain = gain * one(*cut)
    return gain


def gaussian(stream_key, extent, spread, reach, cuts=(), held_as=jnp.bfloat16):
    array = spread * jax.random.normal(stream_key, extent, jnp.float32)
    if cuts:
        array = array * shard_levels(stream_key, extent, cuts, -0.22, 0.18)
    return jnp.clip(array, -reach, reach).astype(held_as)


def setup_inputs(seed: int = 0) -> dict:
    key_list = jax.random.split(jax.random.key(seed), 9)
    forcing = gaussian(key_list[0], (NT, NXE, NYE, EZ, BLOCK), 1.0, 6.0, ((0, 2), (1, 32), (2, 4)), jnp.float32)
    initial = gaussian(key_list[1], (NT, NXE, NYE, EZ, BLOCK), 0.5, 3.0, ((0, 2), (1, 32), (2, 4)), jnp.float32)
    conductance = jnp.clip(jnp.exp(math.log(1.5) - 1.0986123 * jax.random.uniform(key_list[2], (NT, NXE, NYE, EZ), jnp.float32) ** shard_levels(key_list[2], (NT, NXE, NYE, EZ), ((0, 2), (1, 32), (2, 4)), -0.2, 0.2)), 0.5, 1.5)
    counts = draw_counts(jax.random.fold_in(key_list[8], 71), 0)
    block_matrix = draw_block_matrix(jax.random.fold_in(key_list[8], 71), 0)
    precond = draw_precond(jax.random.fold_in(key_list[8], 71), 0)
    face_coupling = gaussian(key_list[6], (6, BLOCK, BLOCK), 32 ** -0.5, 1.0, (), jnp.float32)
    time_coupling = draw_time_coupling(jax.random.fold_in(key_list[8], 71), 0)
    return {"forcing": forcing, "initial": initial, "conductance": conductance, "counts": counts, "block_matrix": block_matrix, "precond": precond, "face_coupling": face_coupling, "time_coupling": time_coupling}


OMEGA = 0.7
precise = lax.Precision.HIGHEST


def product(field, matrix):
    return jnp.einsum("xyzk,kj->xyzj", field, matrix, precision=precise)


def active_mask(counts):
    tiles = jnp.repeat(jnp.repeat(counts, EX, axis=0), EY, axis=1)
    across = lax.broadcasted_iota(jnp.int32, (NXE, NYE, EZ), 0) % EX
    along = lax.broadcasted_iota(jnp.int32, (NXE, NYE, EZ), 1) % EY
    depth_idx = lax.broadcasted_iota(jnp.int32, (NXE, NYE, EZ), 2)
    position = (across * EY + along) * EZ + depth_idx
    return (position < tiles[:, :, None]).astype(jnp.float32)[..., None]


def neighbours(field, face_coupling):
    padded = jnp.pad(field, ((1, 1), (1, 1), (1, 1), (0, 0)))
    pieces = [padded[:-2, 1:-1, 1:-1], padded[2:, 1:-1, 1:-1], padded[1:-1, :-2, 1:-1],
              padded[1:-1, 2:, 1:-1], padded[1:-1, 1:-1, :-2], padded[1:-1, 1:-1, 2:]]
    joined = jnp.concatenate(pieces, axis=-1)
    return product(joined, face_coupling.reshape(6 * BLOCK, BLOCK))


def reference(forcing, initial, conductance, counts, block_matrix, precond, face_coupling, time_coupling):
    active = active_mask(counts)
    mixed = jnp.dot(time_coupling, precond, precision=precise, preferred_element_type=jnp.float32)
    fields = [initial[slab_no] * active for slab_no in range(NT)]
    for sweep_no in range(SWEEPS):
        updated = [None] * NT
        trace_in = jnp.zeros((NXE, NYE, EZ, SPACE), jnp.float32)
        for slab_no in reversed(range(NT)):
            adjoint = fields[slab_no]
            weight = conductance[slab_no][..., None]
            relaxed = OMEGA / weight
            residue = forcing[slab_no] - weight * product(adjoint, block_matrix) - neighbours(adjoint, face_coupling)
            predicted = adjoint + relaxed * product(residue, precond)
            fresh = active * (predicted - relaxed * product(trace_in, mixed))
            updated[slab_no] = fresh
            trace_in = fresh[..., :SPACE]
        fields = updated
    return jnp.stack(fields)
```

```python
import functools

import jax
import jax.numpy as jnp
from jax import lax
from jax.experimental import pallas as pl
from jax.experimental.pallas import tpu as pltpu
from jax.sharding import PartitionSpec as P

SWEEPS = 2
OMEGA = 0.7
NTD, EX, EY, EZ, BLOCK = 4, 8, 16, 16, 128
SPACE = BLOCK // 2
LAYER = EY * EZ
F32, BF16 = jnp.float32, jnp.bfloat16
VMEM = pltpu.VMEM
ANY = pl.BlockSpec(memory_space=pl.ANY)
INV = pl.BlockSpec(memory_space=VMEM)
INS = pl.BlockSpec(memory_space=pltpu.SMEM)
INNER = (1, 6)
OUTER = ((0, 1), (7, 1))


def params(mib):
    return pltpu.CompilerParams(vmem_limit_bytes=mib << 20)


def cost(us):
    return pl.CostEstimate(flops=int(us * 1.0e9), bytes_accessed=0, transcendentals=0)


def split(value):
    high = value.astype(BF16)
    low = (value - high.astype(F32)).astype(BF16)
    return high, low


def dot(rows, matrix):
    return jnp.dot(rows, matrix, preferred_element_type=F32)


def both(value):
    return jnp.concatenate(split(value), axis=-1)


def folded(rows, matrix):
    out = dot(rows, matrix)
    return out[:, :BLOCK] + out[:, BLOCK:]


def mask(info, first, rows):
    position = lax.broadcasted_iota(jnp.int32, (rows, BLOCK), 0) + first * LAYER
    return position < info[0]


def faces_kernel(info, initial, left, right, front, back, sems):
    copies = [
        pltpu.make_async_copy(initial.at[:, 0], left, sems.at[0]),
        pltpu.make_async_copy(initial.at[:, EX - 1], right, sems.at[1]),
        pltpu.make_async_copy(initial.at[:, :, pl.ds(0, EZ)], front, sems.at[2]),
        pltpu.make_async_copy(initial.at[:, :, pl.ds(LAYER - EZ, EZ)], back, sems.at[3]),
    ]
    for copy in copies:
        copy.start()
    for copy, ref, at in zip(copies, (left, right), (0, EX - 1)):
        copy.wait()
        keep = mask(info, at, LAYER)
        for t in range(NTD):
            ref[t] = jnp.where(keep, ref[t], 0.0)
    for copy, ref, at in zip(copies[2:], (front, back), (0, LAYER - EZ)):
        copy.wait()
        for x in range(EX):
            position = lax.broadcasted_iota(jnp.int32, (EZ, BLOCK), 0) + (x * LAYER + at)
            for t in range(NTD):
                ref[t, x] = jnp.where(position < info[0], ref[t, x], 0.0)


def faces_of_initial(info, initial):
    return pl.pallas_call(
        faces_kernel,
        out_shape=[
            VMEM((NTD, LAYER, BLOCK), F32),
            VMEM((NTD, LAYER, BLOCK), F32),
            VMEM((NTD, EX, EZ, BLOCK), F32),
            VMEM((NTD, EX, EZ, BLOCK), F32),
        ],
        in_specs=[INS, ANY],
        out_specs=[INV] * 4,
        scratch_shapes=[pltpu.SemaphoreType.DMA((4,))],
        compiler_params=params(4),
        cost_estimate=cost(2),
        name="faces",
    )(info, initial)


def stencil_setup(high, low):
    for ref in (high, low):
        for x in (0, EX + 1):
            ref[x] = jnp.zeros(ref.shape[1:], BF16)
        for x in range(1, EX + 1):
            for t in range(NTD):
                ref[x, t, 0:EZ] = jnp.zeros((EZ, BLOCK), BF16)
                ref[x, t, EZ + LAYER :] = jnp.zeros((EZ, BLOCK), BF16)


def stencil_split(x, value, high, low):
    h, l = split(value)
    high[x + 1, :, pl.ds(EZ, LAYER)] = h
    low[x + 1, :, pl.ds(EZ, LAYER)] = l


def flat(value):
    return value.reshape(NTD * LAYER, BLOCK)


def stencil_layer(x, adjoint, high, low, lateral, central):
    pieces = []
    for ref in (high, low):
        pieces += [
            flat(ref[x, :, pl.ds(EZ, LAYER)]),
            flat(ref[x + 2, :, pl.ds(EZ, LAYER)]),
            flat(ref[x + 1, :, pl.ds(0, LAYER)]),
            flat(ref[x + 1, :, pl.ds(2 * EZ, LAYER)]),
        ]
    around = folded(jnp.concatenate(pieces, axis=1), lateral[...])
    own = [flat(ref[x + 1, :, pl.ds(EZ, LAYER)]) for ref in (high, low)]
    out = dot(jnp.concatenate(own, axis=1), central[...])
    own, below, above = (
        out[:, k * BLOCK : (k + 1) * BLOCK] + out[:, (k + 3) * BLOCK : (k + 4) * BLOCK] for k in range(3)
    )
    depth = lax.broadcasted_iota(jnp.int32, (NTD * LAYER, BLOCK), 0) % EZ
    below = jnp.where(depth == 0, 0.0, pltpu.roll(below, 1, 0))
    above = jnp.where(depth == EZ - 1, 0.0, pltpu.roll(above, NTD * LAYER - 1, 0))
    return adjoint - own, around + below + above


def first_kernel(
    info, initial, forcing, relaxed, block_matrix, precond, faces, coupling,
    pred, loads, lateral, central, carry,
    adjoint, load, high, low, given, sems,
):
    def fetch(x, which):
        source, target = ((initial, adjoint), (forcing, load))[which]
        return pltpu.make_async_copy(source.at[:, x], target.at[:, x], sems.at[which, x])

    for x in range(EX):
        fetch(x, 0).start()
        fetch(x, 1).start()

    def matrices(value):
        matrix = jnp.dot(value, precond[...], precision=lax.Precision.HIGHEST, preferred_element_type=F32)
        return split(matrix)

    zero = jnp.zeros((BLOCK, BLOCK), BF16)
    for d in range(4):
        h, l = matrices(faces[d])
        lateral[d * BLOCK : (d + 1) * BLOCK, :] = jnp.concatenate([h, l], axis=1)
        lateral[(d + 4) * BLOCK : (d + 5) * BLOCK, :] = jnp.concatenate([h, zero], axis=1)
    parts = [matrices(OMEGA * block_matrix[...]), matrices(faces[4]), matrices(faces[5])]
    central[0:BLOCK, :] = jnp.concatenate([h for h, _ in parts] + [l for _, l in parts], axis=1)
    central[BLOCK:, :] = jnp.concatenate([h for h, _ in parts] + [zero] * 3, axis=1)
    h, l = matrices(coupling[...])
    none = jnp.zeros((SPACE, 2 * BLOCK), BF16)
    carry[...] = jnp.concatenate(
        [jnp.concatenate([h, l], axis=1), none, jnp.concatenate([h, zero[:SPACE]], axis=1), none], axis=0
    )
    h, l = split(precond[...])
    given[0:BLOCK, :] = jnp.concatenate([h, l], axis=1)
    given[BLOCK:, :] = jnp.concatenate([h, zero], axis=1)

    stencil_setup(high, low)

    def enter(x):
        fetch(x, 0).wait()
        position = lax.broadcasted_iota(jnp.int32, (NTD, LAYER, BLOCK), 1) + x * LAYER
        value = jnp.where(position < info[0], adjoint[:, x], 0.0)
        adjoint[:, x] = value
        stencil_split(x, value, high, low)

    def layer(x):
        fetch(x, 1).wait()
        factor = flat(relaxed[:, x])
        rest = factor * folded(both(flat(load[:, x])), given[...])
        loads[:, x] = rest.reshape(NTD, LAYER, BLOCK)
        own, around = stencil_layer(x, flat(adjoint[:, x]), high, low, lateral, central)
        pred[:, x] = (own + rest - factor * around).reshape(NTD, LAYER, BLOCK)

    enter(0)

    def step(x, _):
        enter(x + 1)
        layer(x)
        return 0

    lax.fori_loop(0, EX - 1, step, 0)
    layer(EX - 1)


STACK = (NTD, EX, LAYER, BLOCK)
PADDED = (EX + 2, NTD, LAYER + 2 * EZ, BLOCK)


def first_prediction(info, initial, forcing, relaxed, block_matrix, precond, faces, coupling):
    return pl.pallas_call(
        first_kernel,
        out_shape=[
            VMEM(STACK, F32),
            VMEM(STACK, F32),
            VMEM((8 * BLOCK, 2 * BLOCK), BF16),
            VMEM((2 * BLOCK, 6 * BLOCK), BF16),
            VMEM((2 * BLOCK, 2 * BLOCK), BF16),
        ],
        in_specs=[INS, ANY, ANY] + [INV] * 5,
        out_specs=[INV] * 5,
        scratch_shapes=[
            pltpu.VMEM(STACK, F32),
            pltpu.VMEM(STACK, F32),
            pltpu.VMEM(PADDED, BF16),
            pltpu.VMEM(PADDED, BF16),
            pltpu.VMEM((2 * BLOCK, 2 * BLOCK), BF16),
            pltpu.SemaphoreType.DMA((2, EX)),
        ],
        compiler_params=params(28),
        cost_estimate=cost(10),
        name="first",
    )(info, initial, forcing, relaxed, block_matrix, precond, faces, coupling)


def next_kernel(adjoint, loads, relaxed, lateral, central, pred, high, low):
    stencil_setup(high, low)

    def enter(x):
        stencil_split(x, adjoint[:, x], high, low)

    def layer(x):
        own, around = stencil_layer(x, flat(adjoint[:, x]), high, low, lateral, central)
        value = own + flat(loads[:, x]) - flat(relaxed[:, x]) * around
        pred[:, x] = value.reshape(NTD, LAYER, BLOCK)

    enter(0)

    def step(x, _):
        enter(x + 1)
        layer(x)
        return 0

    lax.fori_loop(0, EX - 1, step, 0)
    layer(EX - 1)


def next_prediction(adjoint, loads, relaxed, lateral, central):
    return pl.pallas_call(
        next_kernel,
        out_shape=VMEM(STACK, F32),
        in_specs=[INV] * 5,
        out_specs=INV,
        scratch_shapes=[pltpu.VMEM(PADDED, BF16), pltpu.VMEM(PADDED, BF16)],
        compiler_params=params(16),
        cost_estimate=cost(8),
        name="next",
    )(adjoint, loads, relaxed, lateral, central)


def chain(info, field, relaxed, carry, runs, incoming):
    traces = incoming
    for t in reversed(range(NTD)):
        fresh = []
        for k, (first, count) in enumerate(runs):
            rows = count * LAYER
            value = field[t, first : first + count].reshape(rows, BLOCK)
            if traces is not None:
                factor = relaxed[t, first : first + count].reshape(rows, BLOCK)
                value = value - factor * folded(both(traces[k]), carry[...])
            value = jnp.where(mask(info, first, rows), value, 0.0)
            field[t, first : first + count] = value.reshape(count, LAYER, BLOCK)
            fresh.append(value)
        traces = fresh
    return traces


def packed(traces):
    if len(traces) == 1:
        half = traces[0].shape[0] // 2
        top, bottom = traces[0][:half], traces[0][half:]
    else:
        top, bottom = traces
    lane = lax.broadcasted_iota(jnp.int32, top.shape, 1)
    return jnp.where(lane < SPACE, top, pltpu.roll(bottom, SPACE, 1))


def unpacked(value, runs):
    swapped = pltpu.roll(value, SPACE, 1)
    if len(runs) == 1:
        return [jnp.concatenate([value, swapped], axis=0)]
    return [value, swapped]


def y_halo_terms(pred, relaxed, lateral, halo, d, at, layers):
    matrix = jnp.concatenate([lateral[d * BLOCK : (d + 1) * BLOCK, :], lateral[(d + 4) * BLOCK : (d + 5) * BLOCK, :]], axis=0)
    first, count = layers
    values = halo[:, first : first + count].reshape(NTD * count * EZ, BLOCK)
    term = folded(both(values), matrix).reshape(NTD, count, EZ, BLOCK)
    rows = pl.ds(at, EZ)
    area = (slice(None), pl.ds(first, count), rows)
    pred[area] = pred[area] - relaxed[area] * term


def inner_kernel(info, pred, relaxed, lateral, carry, front, back, field, trace):
    y_halo_terms(field, relaxed, lateral, front, 2, 0, INNER)
    y_halo_terms(field, relaxed, lateral, back, 3, LAYER - EZ, INNER)

    @pl.when(info[1] == 1)
    def _():
        trace[...] = packed(chain(info, field, relaxed, carry, (INNER,), None))


def x_halo_terms(pred, relaxed, lateral, halo, d, x):
    matrix = jnp.concatenate([lateral[d * BLOCK : (d + 1) * BLOCK, :], lateral[(d + 4) * BLOCK : (d + 5) * BLOCK, :]], axis=0)
    term = folded(both(flat(halo[...])), matrix).reshape(NTD, LAYER, BLOCK)
    pred[:, x] = pred[:, x] - relaxed[:, x] * term


def outer_kernel(info, pred, relaxed, lateral, carry, left, right, front, back, field, trace):
    for run in OUTER:
        y_halo_terms(field, relaxed, lateral, front, 2, 0, run)
        y_halo_terms(field, relaxed, lateral, back, 3, LAYER - EZ, run)
    x_halo_terms(field, relaxed, lateral, left, 0, 0)
    x_halo_terms(field, relaxed, lateral, right, 1, EX - 1)

    @pl.when(info[1] == 1)
    def _():
        trace[...] = packed(chain(info, field, relaxed, carry, OUTER, None))


def with_halos(info, pred, relaxed, lateral, carry, halos, inner):
    rows = (INNER[1] if inner else 2) * LAYER // 2
    return pl.pallas_call(
        inner_kernel if inner else outer_kernel,
        out_shape=[VMEM(STACK, F32), VMEM((rows, BLOCK), F32)],
        in_specs=[INS] + [INV] * (4 + len(halos)),
        out_specs=[INV, INV],
        input_output_aliases={1: 0},
        compiler_params=params(8),
        cost_estimate=cost(2),
        name="halo_inner" if inner else "halo_outer",
    )(info, pred, relaxed, lateral, carry, *halos)


def late_chain(info, field, relaxed, carry, trace, runs):
    @pl.when(info[1] == 0)
    def _():
        chain(info, field, relaxed, carry, runs, unpacked(trace[...], runs))


def late_inner_kernel(info, field, relaxed, carry, trace, out):
    late_chain(info, out, relaxed, carry, trace, (INNER,))


def late_outer_kernel(info, field, relaxed, carry, trace, out, left, right, front, back):
    late_chain(info, out, relaxed, carry, trace, OUTER)
    left[...] = out[:, 0]
    right[...] = out[:, EX - 1]
    front[...] = out[:, :, pl.ds(0, EZ)]
    back[...] = out[:, :, pl.ds(LAYER - EZ, EZ)]


def after_trace(info, field, relaxed, carry, trace, inner):
    out_shape = [VMEM(STACK, F32)]
    if not inner:
        out_shape += [VMEM((NTD, LAYER, BLOCK), F32)] * 2 + [VMEM((NTD, EX, EZ, BLOCK), F32)] * 2
    return pl.pallas_call(
        late_inner_kernel if inner else late_outer_kernel,
        out_shape=out_shape,
        in_specs=[INS] + [INV] * 4,
        out_specs=[INV] * len(out_shape),
        input_output_aliases={1: 0},
        compiler_params=params(8),
        cost_estimate=cost(2),
        name="late_inner" if inner else "late_outer",
    )(info, field, relaxed, carry, trace)


def last_inner_kernel(info, field, relaxed, carry, trace, kept, out, sem):
    late_chain(info, kept, relaxed, carry, trace, (INNER,))
    first, count = INNER
    copy = pltpu.make_async_copy(kept.at[:, pl.ds(first, count)], out.at[:, pl.ds(first, count)], sem)
    copy.start()
    copy.wait()


def last_outer_kernel(info, field, relaxed, carry, trace, given, kept, out, sems):
    late_chain(info, kept, relaxed, carry, trace, OUTER)
    copies = [
        pltpu.make_async_copy(kept.at[:, x], out.at[:, x], sems.at[k]) for k, (x, _) in enumerate(OUTER)
    ]
    for copy in copies:
        copy.start()
    for copy in copies:
        copy.wait()


def last_inner(info, field, relaxed, carry, trace):
    return pl.pallas_call(
        last_inner_kernel,
        out_shape=[VMEM(STACK, F32), jax.ShapeDtypeStruct(STACK, F32)],
        in_specs=[INS] + [INV] * 4,
        out_specs=[INV, ANY],
        input_output_aliases={1: 0},
        scratch_shapes=[pltpu.SemaphoreType.DMA],
        compiler_params=params(8),
        cost_estimate=cost(3),
        name="last_inner",
    )(info, field, relaxed, carry, trace)


def last_outer(info, field, relaxed, carry, trace, given):
    return pl.pallas_call(
        last_outer_kernel,
        out_shape=[VMEM(STACK, F32), jax.ShapeDtypeStruct(STACK, F32)],
        in_specs=[INS] + [INV] * 4 + [ANY],
        out_specs=[INV, ANY],
        input_output_aliases={1: 0, 5: 1},
        scratch_shapes=[pltpu.SemaphoreType.DMA((2,))],
        compiler_params=params(8),
        cost_estimate=cost(2),
        name="last_outer",
    )(info, field, relaxed, carry, trace, given)[1]


def shifted(value, axis, step):
    count = lax.axis_size(axis)
    first, last = max(0, -step), min(count, count - step)
    return lax.ppermute(value, axis, [(i, i + step) for i in range(first, last)])


def halos_of(faces):
    left, right, front, back = faces
    return (shifted(right, "sx", 1), shifted(left, "sx", -1), shifted(back, "sy", 1), shifted(front, "sy", -1))


def body(forcing, initial, conductance, counts, block_matrix, precond, face_coupling, time_coupling):
    shape = forcing.shape
    forcing, initial = forcing.reshape(STACK), initial.reshape(STACK)
    info = jnp.stack([counts[0, 0], lax.axis_index("tm").astype(jnp.int32)])
    relaxed = jnp.broadcast_to((OMEGA / conductance).reshape(NTD, EX, LAYER, 1), STACK)
    halos = halos_of(faces_of_initial(info, initial))
    field, loads, lateral, central, carry = first_prediction(
        info, initial, forcing, relaxed, block_matrix, precond, face_coupling, time_coupling
    )
    for sweep in range(SWEEPS):
        if sweep:
            field = next_prediction(field, loads, relaxed, lateral, central)
        field, inner = with_halos(info, field, relaxed, lateral, carry, halos[2:], True)
        inner = shifted(inner, "tm", -1)
        field, outer = with_halos(info, field, relaxed, lateral, carry, halos, False)
        outer = shifted(outer, "tm", -1)
        if sweep < SWEEPS - 1:
            (field,) = after_trace(info, field, relaxed, carry, inner, True)
            field, *faces = after_trace(info, field, relaxed, carry, outer, False)
            halos = halos_of(faces)
        else:
            field, out = last_inner(info, field, relaxed, carry, inner)
            out = last_outer(info, field, relaxed, carry, outer, out)
    return out.reshape(shape)


def solution(mesh):
    in_specs = (
        P("tm", "sx", "sy", None, None),
        P("tm", "sx", "sy", None, None),
        P("tm", "sx", "sy", None),
        P("sx", "sy"),
        P(),
        P(),
        P(),
        P(),
    )
    out_specs = P("tm", "sx", "sy", None, None)
    return jax.shard_map(body, mesh=mesh, in_specs=in_specs, out_specs=out_specs, check_vma=False)
```

```python
import functools

import jax
import jax.numpy as jnp
from jax import lax
from jax.experimental import pallas as pl
from jax.experimental.pallas import tpu as pltpu
from jax.sharding import PartitionSpec as P

SWEEPS = 2
OMEGA = 0.7
NTD, EX, EY, EZ, BLOCK = 4, 8, 16, 16, 128
SPACE = BLOCK // 2
LAYER = EY * EZ
F32, BF16 = jnp.float32, jnp.bfloat16
VMEM = pltpu.VMEM
ANY = pl.BlockSpec(memory_space=pl.ANY)
INH = pl.BlockSpec(memory_space=pltpu.HBM)
INV = pl.BlockSpec(memory_space=VMEM)
INS = pl.BlockSpec(memory_space=pltpu.SMEM)
INNER = ((1, 4),)
OUTER = ((0, 1), (5, 3))


def params(mib):
    return pltpu.CompilerParams(vmem_limit_bytes=mib << 20)


def cost(us):
    return pl.CostEstimate(flops=int(us * 1.0e9), bytes_accessed=0, transcendentals=0)


def split(value):
    high = value.astype(BF16)
    low = (value - high.astype(F32)).astype(BF16)
    return high, low


def dot(rows, matrix):
    return jnp.dot(rows, matrix, preferred_element_type=F32)


def both(value):
    return jnp.concatenate(split(value), axis=-1)


def folded(rows, matrix):
    out = dot(rows, matrix)
    return out[:, :BLOCK] + out[:, BLOCK:]


def mask(info, first, rows):
    position = lax.broadcasted_iota(jnp.int32, (rows, BLOCK), 0) + first * LAYER
    return position < info[0]


def near(info, dim):
    return pl.multiple_of(info[3], EZ) if dim else info[2]


def far(info, dim):
    return pl.multiple_of(LAYER - EZ - info[3], EZ) if dim else EX - 1 - info[2]


def faces_kernel(info, initial, x_near, x_far, y_near, y_far, sems):
    places = (near(info, 0), far(info, 0), near(info, 1), far(info, 1))
    refs = (x_near, x_far, y_near, y_far)
    copies = [
        pltpu.make_async_copy(initial.at[:, at] if k < 2 else initial.at[:, :, pl.ds(at, EZ)], ref, sems.at[k])
        for k, (ref, at) in enumerate(zip(refs, places))
    ]
    for copy in copies:
        copy.start()
    for copy, ref, at in zip(copies[:2], refs[:2], places[:2]):
        copy.wait()
        keep = mask(info, at, LAYER)
        for t in range(NTD):
            ref[t] = jnp.where(keep, ref[t], 0.0)
    for copy, ref, at in zip(copies[2:], refs[2:], places[2:]):
        copy.wait()
        for x in range(EX):
            position = lax.broadcasted_iota(jnp.int32, (EZ, BLOCK), 0) + (x * LAYER + at)
            for t in range(NTD):
                ref[t, x] = jnp.where(position < info[0], ref[t, x], 0.0)


FACES = [VMEM((NTD, LAYER, BLOCK), F32)] * 2 + [VMEM((NTD, EX, EZ, BLOCK), F32)] * 2


def faces_of_initial(info, initial):
    return pl.pallas_call(
        faces_kernel,
        out_shape=FACES,
        in_specs=[INS, INH],
        out_specs=[INV] * 4,
        scratch_shapes=[pltpu.SemaphoreType.DMA((4,))],
        compiler_params=params(4),
        cost_estimate=cost(2),
        name="faces",
    )(info, initial)


def stencil_setup(high, low):
    for ref in (high, low):
        for x in (0, EX + 1):
            ref[x] = jnp.zeros(ref.shape[1:], BF16)
        for x in range(1, EX + 1):
            for t in range(NTD):
                ref[x, t, 0:EZ] = jnp.zeros((EZ, BLOCK), BF16)
                ref[x, t, EZ + LAYER :] = jnp.zeros((EZ, BLOCK), BF16)


def stencil_split(x, value, high, low):
    h, l = split(value)
    high[x + 1, :, pl.ds(EZ, LAYER)] = h
    low[x + 1, :, pl.ds(EZ, LAYER)] = l


def flat(value):
    return value.reshape(NTD * LAYER, BLOCK)


def stencil_layer(x, adjoint, high, low, lateral, central):
    pieces = []
    for ref in (high, low):
        pieces += [
            flat(ref[x, :, pl.ds(EZ, LAYER)]),
            flat(ref[x + 2, :, pl.ds(EZ, LAYER)]),
            flat(ref[x + 1, :, pl.ds(0, LAYER)]),
            flat(ref[x + 1, :, pl.ds(2 * EZ, LAYER)]),
        ]
    around = folded(jnp.concatenate(pieces, axis=1), lateral[...])
    own = [flat(ref[x + 1, :, pl.ds(EZ, LAYER)]) for ref in (high, low)]
    out = dot(jnp.concatenate(own, axis=1), central[...])
    own, below, above = (
        out[:, k * BLOCK : (k + 1) * BLOCK] + out[:, (k + 3) * BLOCK : (k + 4) * BLOCK] for k in range(3)
    )
    depth = lax.broadcasted_iota(jnp.int32, (NTD * LAYER, BLOCK), 0) % EZ
    below = jnp.where(depth == 0, 0.0, pltpu.roll(below, 1, 0))
    above = jnp.where(depth == EZ - 1, 0.0, pltpu.roll(above, NTD * LAYER - 1, 0))
    return adjoint - own, around + below + above


STACK = (NTD, EX, LAYER, BLOCK)
PADDED = (EX + 2, NTD, LAYER + 2 * EZ, BLOCK)
LATERAL = (8 * BLOCK, 2 * BLOCK)
CENTRAL = (2 * BLOCK, 6 * BLOCK)
SQUARE = (2 * BLOCK, 2 * BLOCK)


def layers(runs):
    return [x for first, count in runs for x in range(first, first + count)]


def row_factors(conductance, x, relaxed):
    factor = []
    for t in range(NTD):
        inverse = OMEGA / conductance[t, x]
        spread = jnp.broadcast_to(inverse[:, None, :], (EY, EZ, EZ)).reshape(LAYER, EZ)
        lane = lax.broadcasted_iota(jnp.int32, (LAYER, EZ), 1)
        depth = lax.broadcasted_iota(jnp.int32, (LAYER, EZ), 0) % EZ
        column = jnp.sum(jnp.where(lane == depth, spread, 0.0), axis=1, keepdims=True)
        column = jnp.broadcast_to(column, (LAYER, BLOCK))
        relaxed[t, x] = column
        factor.append(column)
    return jnp.concatenate(factor, axis=0)


def predict(x, field, adjoint, loads, relaxed, high, low, lateral, central, given=None, conductance=None):
    if given is None:
        factor, rest = flat(relaxed[:, x]), flat(loads[:, x])
    else:
        factor = row_factors(conductance, x, relaxed)
        rest = factor * folded(both(flat(loads[:, x])), given[...])
        loads[:, x] = rest.reshape(NTD, LAYER, BLOCK)
    own, around = stencil_layer(x, flat(adjoint[:, x]), high, low, lateral, central)
    field[:, x] = (own + rest - factor * around).reshape(NTD, LAYER, BLOCK)


def first_kernel(
    info, initial, forcing, conductance, block_matrix_hbm, precond_hbm, faces_hbm, coupling_hbm,
    field, adjoint, loads, relaxed, high, low, lateral, central, carry, given,
    block_matrix, precond, faces, coupling, sems, small_sems,
):
    small = [
        pltpu.make_async_copy(source, target, small_sems.at[k])
        for k, (source, target) in enumerate(
            [(precond_hbm, precond), (faces_hbm, faces), (block_matrix_hbm, block_matrix), (coupling_hbm, coupling)]
        )
    ]
    for copy in small:
        copy.start()

    def fetch(x, which):
        source, target = ((initial, adjoint), (forcing, loads))[which]
        return pltpu.make_async_copy(source.at[:, x], target.at[:, x], sems.at[which, x])

    order = layers(INNER) + layers(OUTER)
    for which in range(2):
        for x in order:
            fetch(x, which).start()
    stencil_setup(high, low)
    for copy in small:
        copy.wait()

    def matrices(value):
        matrix = jnp.dot(value, precond[...], precision=lax.Precision.HIGHEST, preferred_element_type=F32)
        return split(matrix)

    zero = jnp.zeros((BLOCK, BLOCK), BF16)
    for d in range(4):
        h, l = matrices(faces[d])
        lateral[d * BLOCK : (d + 1) * BLOCK, :] = jnp.concatenate([h, l], axis=1)
        lateral[(d + 4) * BLOCK : (d + 5) * BLOCK, :] = jnp.concatenate([h, zero], axis=1)
    parts = [matrices(OMEGA * block_matrix[...]), matrices(faces[4]), matrices(faces[5])]
    central[0:BLOCK, :] = jnp.concatenate([h for h, _ in parts] + [l for _, l in parts], axis=1)
    central[BLOCK:, :] = jnp.concatenate([h for h, _ in parts] + [zero] * 3, axis=1)
    h, l = matrices(coupling[...])
    none = jnp.zeros((SPACE, 2 * BLOCK), BF16)
    carry[...] = jnp.concatenate(
        [jnp.concatenate([h, l], axis=1), none, jnp.concatenate([h, zero[:SPACE]], axis=1), none], axis=0
    )
    h, l = split(precond[...])
    given[0:BLOCK, :] = jnp.concatenate([h, l], axis=1)
    given[BLOCK:, :] = jnp.concatenate([h, zero], axis=1)

    for x in range(EX):
        fetch(x, 0).wait()
        position = lax.broadcasted_iota(jnp.int32, (NTD, LAYER, BLOCK), 1) + x * LAYER
        value = jnp.where(position < info[0], adjoint[:, x], 0.0)
        adjoint[:, x] = value
        stencil_split(x, value, high, low)
    for x in range(EX):
        fetch(x, 1).wait()
    for x in layers(INNER):
        predict(x, field, adjoint, loads, relaxed, high, low, lateral, central, given, conductance)


def first_prediction(info, initial, forcing, conductance, block_matrix, precond, faces, coupling):
    return pl.pallas_call(
        first_kernel,
        out_shape=[VMEM(STACK, F32)] * 4
        + [VMEM(PADDED, BF16)] * 2
        + [VMEM(LATERAL, BF16), VMEM(CENTRAL, BF16), VMEM(SQUARE, BF16), VMEM(SQUARE, BF16)],
        in_specs=[INS, INH, INH, INV] + [INH] * 4,
        out_specs=[INV] * 10,
        scratch_shapes=[
            pltpu.VMEM((BLOCK, BLOCK), F32),
            pltpu.VMEM((BLOCK, BLOCK), F32),
            pltpu.VMEM((6, BLOCK, BLOCK), F32),
            pltpu.VMEM((SPACE, BLOCK), F32),
            pltpu.SemaphoreType.DMA((2, EX)),
            pltpu.SemaphoreType.DMA((4,)),
        ],
        compiler_params=params(16),
        cost_estimate=cost(8),
        name="first_inner",
    )(info, initial, forcing, conductance, block_matrix, precond, faces, coupling)


def next_kernel(adjoint, loads, relaxed, lateral, central, field, high, low):
    stencil_setup(high, low)
    for x in range(EX):
        stencil_split(x, adjoint[:, x], high, low)
    for x in layers(INNER):
        predict(x, field, adjoint, loads, relaxed, high, low, lateral, central)


def next_prediction(adjoint, loads, relaxed, lateral, central):
    return pl.pallas_call(
        next_kernel,
        out_shape=[VMEM(STACK, F32), VMEM(PADDED, BF16), VMEM(PADDED, BF16)],
        in_specs=[INV] * 5,
        out_specs=[INV] * 3,
        compiler_params=params(16),
        cost_estimate=cost(5),
        name="next_inner",
    )(adjoint, loads, relaxed, lateral, central)


def rows_of(stack, t, runs):
    return jnp.concatenate([stack[t, first : first + count].reshape(count * LAYER, BLOCK) for first, count in runs], axis=0)


def chain(info, field, relaxed, carry, runs, trace):
    keep = jnp.concatenate(
        [
            (lax.broadcasted_iota(jnp.int32, (count * LAYER, BLOCK), 0) + first * LAYER < info[0]).astype(F32)
            for first, count in runs
        ],
        axis=0,
    ) > 0.5
    for t in reversed(range(NTD)):
        value = rows_of(field, t, runs)
        if trace is not None:
            value = value - rows_of(relaxed, t, runs) * folded(both(trace), carry[...])
        trace = jnp.where(keep, value, 0.0)
        at = 0
        for first, count in runs:
            rows = count * LAYER
            field[t, first : first + count] = trace[at : at + rows].reshape(count, LAYER, BLOCK)
            at += rows
    return trace


def packed(trace):
    half = trace.shape[0] // 2
    lane = lax.broadcasted_iota(jnp.int32, (half, BLOCK), 1)
    return jnp.where(lane < SPACE, trace[:half], pltpu.roll(trace[half:], SPACE, 1))


def unpacked(value):
    return jnp.concatenate([value, pltpu.roll(value, SPACE, 1)], axis=0)


def trace_shape(runs):
    return VMEM((len(layers(runs)) * LAYER // 2, BLOCK), F32)


def early_chain(info, field, relaxed, carry, runs, trace):
    @pl.when(info[1] == 1)
    def _():
        trace[...] = packed(chain(info, field, relaxed, carry, runs, None))


def face_matrix(lateral, d):
    top, bottom = pl.multiple_of(d * BLOCK, BLOCK), pl.multiple_of((d + 4) * BLOCK, BLOCK)
    return jnp.concatenate([lateral[pl.ds(top, BLOCK), :], lateral[pl.ds(bottom, BLOCK), :]], axis=0)


def inner_kernel(info, pred, relaxed, lateral, carry, y_near, y_far, field, trace):
    ((first, count),) = INNER
    for halo, at in ((y_near, near(info, 1)), (y_far, far(info, 1))):
        matrix = face_matrix(lateral, 2 + (at > 0).astype(jnp.int32))
        values = halo[:, first : first + count].reshape(NTD * count * EZ, BLOCK)
        term = folded(both(values), matrix).reshape(NTD, count, EZ, BLOCK)
        area = (slice(None), pl.ds(first, count), pl.ds(at, EZ))
        field[area] = field[area] - relaxed[area] * term
    early_chain(info, field, relaxed, carry, INNER, trace)


def inner_halos(info, field, relaxed, lateral, carry, y_halos):
    return pl.pallas_call(
        inner_kernel,
        out_shape=[VMEM(STACK, F32), trace_shape(INNER)],
        in_specs=[INS] + [INV] * 6,
        out_specs=[INV, INV],
        input_output_aliases={1: 0},
        compiler_params=params(8),
        cost_estimate=cost(2),
        name="inner_halos",
    )(info, field, relaxed, lateral, carry, *y_halos)


def outer_kernel(first_sweep, info, *refs):
    if first_sweep:
        conductance, given, *refs = refs
        (_, _, _, _, _, adjoint, lateral, central, carry, x_near, x_far, y_near, y_far,
         field, high, low, loads, relaxed, trace) = refs
    else:
        conductance = given = None
        (_, _, _, adjoint, lateral, central, carry, x_near, x_far, y_near, y_far, loads, relaxed,
         field, high, low, trace) = refs
    for halo, x in ((x_near, near(info, 0)), (x_far, far(info, 0))):
        h, l = split(halo[...])
        place = jnp.where(x > 0, EX + 1, 0)
        high[place, :, pl.ds(EZ, LAYER)] = h
        low[place, :, pl.ds(EZ, LAYER)] = l
    for halo, y in ((y_near, near(info, 1)), (y_far, far(info, 1))):
        place = pl.multiple_of(jnp.where(y > 0, LAYER + EZ, 0), EZ)
        for x in layers(OUTER):
            h, l = split(halo[:, x])
            high[x + 1, :, pl.ds(place, EZ)] = h
            low[x + 1, :, pl.ds(place, EZ)] = l
    for x in layers(OUTER):
        predict(x, field, adjoint, loads, relaxed, high, low, lateral, central, given, conductance)
    early_chain(info, field, relaxed, carry, OUTER, trace)


def outer_prediction(info, field, high, low, adjoint, lateral, central, carry, halos, loads, relaxed, given, conductance):
    first_sweep = given is not None
    if first_sweep:
        args = [info, conductance, given, field, high, low, loads, relaxed, adjoint, lateral, central, carry, *halos]
        outs = [VMEM(STACK, F32), VMEM(PADDED, BF16), VMEM(PADDED, BF16), VMEM(STACK, F32), VMEM(STACK, F32)]
        aliases = {k + 3: k for k in range(5)}
    else:
        args = [info, field, high, low, adjoint, lateral, central, carry, *halos, loads, relaxed]
        outs = [VMEM(STACK, F32), VMEM(PADDED, BF16), VMEM(PADDED, BF16)]
        aliases = {k + 1: k for k in range(3)}
    outs = outs + [trace_shape(OUTER)]
    out = pl.pallas_call(
        functools.partial(outer_kernel, first_sweep),
        out_shape=outs,
        in_specs=[INS] + [INV] * (len(args) - 1),
        out_specs=[INV] * len(outs),
        input_output_aliases=aliases,
        compiler_params=params(16),
        cost_estimate=cost(7),
        name="first_outer" if first_sweep else "next_outer",
    )(*args)
    if first_sweep:
        loads, relaxed = out[3:5]
    return out[0], out[-1], loads, relaxed


def late_chain(info, field, relaxed, carry, trace, runs):
    @pl.when(info[1] == 0)
    def _():
        chain(info, field, relaxed, carry, runs, unpacked(trace[...]))


def late_inner_kernel(info, field, relaxed, carry, trace, out):
    late_chain(info, out, relaxed, carry, trace, INNER)


def late_outer_kernel(info, field, relaxed, carry, trace, out, x_near, x_far, y_near, y_far):
    late_chain(info, out, relaxed, carry, trace, OUTER)
    x_near[...] = out[:, near(info, 0)]
    x_far[...] = out[:, far(info, 0)]
    y_near[...] = out[:, :, pl.ds(near(info, 1), EZ)]
    y_far[...] = out[:, :, pl.ds(far(info, 1), EZ)]


def after_trace(info, field, relaxed, carry, trace, inner):
    outs = [VMEM(STACK, F32)] + ([] if inner else FACES)
    return pl.pallas_call(
        late_inner_kernel if inner else late_outer_kernel,
        out_shape=outs,
        in_specs=[INS] + [INV] * 4,
        out_specs=[INV] * len(outs),
        input_output_aliases={1: 0},
        compiler_params=params(8),
        cost_estimate=cost(2),
        name="late_inner" if inner else "late_outer",
    )(info, field, relaxed, carry, trace)


def finish(runs, kept, out, sems):
    copies = [
        pltpu.make_async_copy(kept.at[:, pl.ds(first, count)], out.at[:, pl.ds(first, count)], sems.at[k])
        for k, (first, count) in enumerate(runs)
    ]
    for copy in copies:
        copy.start()
    for copy in copies:
        copy.wait()


def last_inner_kernel(info, field, relaxed, carry, trace, kept, out, sems):
    late_chain(info, kept, relaxed, carry, trace, INNER)
    finish(INNER, kept, out, sems)


def last_outer_kernel(info, field, relaxed, carry, trace, given, kept, out, sems):
    late_chain(info, kept, relaxed, carry, trace, OUTER)
    finish(OUTER, kept, out, sems)


def last(info, field, relaxed, carry, trace, given):
    inner = given is None
    args = [info, field, relaxed, carry, trace] + ([] if inner else [given])
    return pl.pallas_call(
        last_inner_kernel if inner else last_outer_kernel,
        out_shape=[VMEM(STACK, F32), pltpu.HBM(STACK, F32)],
        in_specs=[INS] + [INV] * 4 + ([] if inner else [INH]),
        out_specs=[INV, INH],
        input_output_aliases={1: 0} if inner else {1: 0, 5: 1},
        scratch_shapes=[pltpu.SemaphoreType.DMA((2,))],
        compiler_params=params(8),
        cost_estimate=cost(3),
        name="last_inner" if inner else "last_outer",
    )(*args)


def exchanged(value, axis, first):
    count = lax.axis_size(axis)
    pairs = [(i, i + 1) for i in range(first, count - 1, 2)]
    return lax.ppermute(value, axis, pairs + [(j, i) for i, j in pairs])


def sent_back(value):
    return lax.ppermute(value, "tm", [(1, 0)])


def body(forcing, initial, conductance, counts, block_matrix, precond, face_coupling, time_coupling):
    shape = forcing.shape
    in_hbm = functools.partial(pltpu.with_memory_space_constraint, memory_space=pltpu.HBM)
    forcing, initial = in_hbm(forcing.reshape(STACK)), in_hbm(initial.reshape(STACK))
    block_matrix, precond, face_coupling, time_coupling = map(
        in_hbm, (block_matrix, precond, face_coupling, time_coupling)
    )
    even_x = 1 - lax.rem(lax.axis_index("sx"), 2).astype(jnp.int32)
    even_y = 1 - lax.rem(lax.axis_index("sy"), 2).astype(jnp.int32)
    info = jnp.stack(
        [counts[0, 0], lax.axis_index("tm").astype(jnp.int32), even_x * (EX - 1), even_y * (LAYER - EZ)]
    )

    def halos_of(x_near, x_far, y_near, y_far):
        return (
            exchanged(x_near, "sx", 0), exchanged(x_far, "sx", 1),
            exchanged(y_near, "sy", 0), exchanged(y_far, "sy", 1),
        )

    halos = halos_of(*faces_of_initial(info, initial))
    field, adjoint, loads, relaxed, high, low, lateral, central, carry, given = first_prediction(
        info, initial, forcing, conductance, block_matrix, precond, face_coupling, time_coupling
    )
    for sweep in range(SWEEPS):
        if sweep:
            adjoint, given = field, None
            field, high, low = next_prediction(adjoint, loads, relaxed, lateral, central)
        field, inner = inner_halos(info, field, relaxed, lateral, carry, halos[2:])
        inner = sent_back(inner)
        field, outer, loads, relaxed = outer_prediction(
            info, field, high, low, adjoint, lateral, central, carry, halos, loads, relaxed, given, conductance
        )
        outer = sent_back(outer)
        if sweep < SWEEPS - 1:
            (field,) = after_trace(info, field, relaxed, carry, inner, True)
            field, *faces = after_trace(info, field, relaxed, carry, outer, False)
            halos = halos_of(*faces)
        else:
            field, out = last(info, field, relaxed, carry, inner, None)
            field, out = last(info, field, relaxed, carry, outer, out)
    return out.reshape(shape)


def solution(mesh):
    in_specs = (
        P("tm", "sx", "sy", None, None),
        P("tm", "sx", "sy", None, None),
        P("tm", "sx", "sy", None),
        P("sx", "sy"),
        P(),
        P(),
        P(),
        P(),
    )
    out_specs = P("tm", "sx", "sy", None, None)
    return jax.shard_map(body, mesh=mesh, in_specs=in_specs, out_specs=out_specs, check_vma=False)
```

```python
import functools

import jax
import jax.numpy as jnp
from jax import lax
from jax.experimental import pallas as pl
from jax.experimental.pallas import tpu as pltpu
from jax.sharding import PartitionSpec as P

SWEEPS = 2
OMEGA = 0.7
NTD, EX, EY, EZ, BLOCK = 4, 8, 16, 16, 128
SPACE = BLOCK // 2
LAYER = EY * EZ
F32, BF16 = jnp.float32, jnp.bfloat16
VMEM = pltpu.VMEM
ANY = pl.BlockSpec(memory_space=pl.ANY)
INH = pl.BlockSpec(memory_space=pltpu.HBM)
INV = pl.BlockSpec(memory_space=VMEM)
INS = pl.BlockSpec(memory_space=pltpu.SMEM)
INNER = ((1, 5),)
OUTER = ((0, 1), (6, 2))


def params(mib):
    return pltpu.CompilerParams(vmem_limit_bytes=mib << 20)


def cost(us):
    return pl.CostEstimate(flops=int(us * 1.0e9), bytes_accessed=0, transcendentals=0)


def split(value):
    high = value.astype(BF16)
    low = (value - high.astype(F32)).astype(BF16)
    return high, low


def dot(rows, matrix):
    return jnp.dot(rows, matrix, preferred_element_type=F32)


def both(value):
    return jnp.concatenate(split(value), axis=-1)


def folded(rows, matrix):
    out = dot(rows, matrix)
    return out[:, :BLOCK] + out[:, BLOCK:]


def mask(info, first, rows):
    position = lax.broadcasted_iota(jnp.int32, (rows, BLOCK), 0) + first * LAYER
    return position < info[0]


def near(info, dim):
    return pl.multiple_of(info[3], EZ) if dim else info[2]


def far(info, dim):
    return pl.multiple_of(LAYER - EZ - info[3], EZ) if dim else EX - 1 - info[2]


def faces_kernel(info, initial, x_near, x_far, y_near, y_far, sems):
    places = (near(info, 0), far(info, 0), near(info, 1), far(info, 1))
    refs = (x_near, x_far, y_near, y_far)
    copies = [
        pltpu.make_async_copy(initial.at[:, at] if k < 2 else initial.at[:, :, pl.ds(at, EZ)], ref, sems.at[k])
        for k, (ref, at) in enumerate(zip(refs, places))
    ]
    for copy in copies:
        copy.start()
    for copy, ref, at in zip(copies[:2], refs[:2], places[:2]):
        copy.wait()
        keep = mask(info, at, LAYER)
        for t in range(NTD):
            ref[t] = jnp.where(keep, ref[t], 0.0)
    for copy, ref, at in zip(copies[2:], refs[2:], places[2:]):
        copy.wait()
        for x in range(EX):
            position = lax.broadcasted_iota(jnp.int32, (EZ, BLOCK), 0) + (x * LAYER + at)
            for t in range(NTD):
                ref[t, x] = jnp.where(position < info[0], ref[t, x], 0.0)


FACES = [VMEM((NTD, LAYER, BLOCK), F32)] * 2 + [VMEM((NTD, EX, EZ, BLOCK), F32)] * 2


def faces_of_initial(info, initial):
    return pl.pallas_call(
        faces_kernel,
        out_shape=FACES,
        in_specs=[INS, INH],
        out_specs=[INV] * 4,
        scratch_shapes=[pltpu.SemaphoreType.DMA((4,))],
        compiler_params=params(4),
        cost_estimate=cost(2),
        name="faces",
    )(info, initial)


def stencil_setup(high, low):
    for ref in (high, low):
        for x in (0, EX + 1):
            ref[x] = jnp.zeros(ref.shape[1:], BF16)
        for x in range(1, EX + 1):
            for t in range(NTD):
                ref[x, t, 0:EZ] = jnp.zeros((EZ, BLOCK), BF16)
                ref[x, t, EZ + LAYER :] = jnp.zeros((EZ, BLOCK), BF16)


def stencil_split(x, value, high, low):
    h, l = split(value)
    high[x + 1, :, pl.ds(EZ, LAYER)] = h
    low[x + 1, :, pl.ds(EZ, LAYER)] = l


def flat(value):
    return value.reshape(NTD * LAYER, BLOCK)


def stencil_layer(x, adjoint, high, low, lateral, central):
    pieces = []
    for ref in (high, low):
        pieces += [
            flat(ref[x, :, pl.ds(EZ, LAYER)]),
            flat(ref[x + 2, :, pl.ds(EZ, LAYER)]),
            flat(ref[x + 1, :, pl.ds(0, LAYER)]),
            flat(ref[x + 1, :, pl.ds(2 * EZ, LAYER)]),
        ]
    around = folded(jnp.concatenate(pieces, axis=1), lateral[...])
    own = [flat(ref[x + 1, :, pl.ds(EZ, LAYER)]) for ref in (high, low)]
    out = dot(jnp.concatenate(own, axis=1), central[...])
    own, below, above = (
        out[:, k * BLOCK : (k + 1) * BLOCK] + out[:, (k + 3) * BLOCK : (k + 4) * BLOCK] for k in range(3)
    )
    depth = lax.broadcasted_iota(jnp.int32, (NTD * LAYER, BLOCK), 0) % EZ
    below = jnp.where(depth == 0, 0.0, pltpu.roll(below, 1, 0))
    above = jnp.where(depth == EZ - 1, 0.0, pltpu.roll(above, NTD * LAYER - 1, 0))
    return adjoint - own, around + below + above


STACK = (NTD, EX, LAYER, BLOCK)
PADDED = (EX + 2, NTD, LAYER + 2 * EZ, BLOCK)
LATERAL = (8 * BLOCK, 2 * BLOCK)
CENTRAL = (2 * BLOCK, 6 * BLOCK)
SQUARE = (2 * BLOCK, 2 * BLOCK)


def layers(runs):
    return [x for first, count in runs for x in range(first, first + count)]


def row_factors(conductance, x, relaxed):
    factor = []
    for t in range(NTD):
        inverse = OMEGA / conductance[t, x]
        spread = jnp.broadcast_to(inverse[:, None, :], (EY, EZ, EZ)).reshape(LAYER, EZ)
        lane = lax.broadcasted_iota(jnp.int32, (LAYER, EZ), 1)
        depth = lax.broadcasted_iota(jnp.int32, (LAYER, EZ), 0) % EZ
        column = jnp.sum(jnp.where(lane == depth, spread, 0.0), axis=1, keepdims=True)
        column = jnp.broadcast_to(column, (LAYER, BLOCK))
        relaxed[t, x] = column
        factor.append(column)
    return jnp.concatenate(factor, axis=0)


def predict(x, field, adjoint, loads, relaxed, high, low, lateral, central, given=None, conductance=None):
    if given is None:
        factor, rest = flat(relaxed[:, x]), flat(loads[:, x])
    else:
        factor = row_factors(conductance, x, relaxed)
        rest = factor * folded(both(flat(loads[:, x])), given[...])
        loads[:, x] = rest.reshape(NTD, LAYER, BLOCK)
    own, around = stencil_layer(x, flat(adjoint[:, x]), high, low, lateral, central)
    field[:, x] = (own + rest - factor * around).reshape(NTD, LAYER, BLOCK)


def first_kernel(
    info, initial, forcing, conductance, block_matrix_hbm, precond_hbm, faces_hbm, coupling_hbm,
    field, adjoint, loads, relaxed, high, low, lateral, central, carry, given,
    block_matrix, precond, faces, coupling, sems, small_sems,
):
    small = [
        pltpu.make_async_copy(source, target, small_sems.at[k])
        for k, (source, target) in enumerate(
            [(precond_hbm, precond), (faces_hbm, faces), (block_matrix_hbm, block_matrix), (coupling_hbm, coupling)]
        )
    ]
    for copy in small:
        copy.start()

    def fetch(x, which):
        source, target = ((initial, adjoint), (forcing, loads))[which]
        return pltpu.make_async_copy(source.at[:, x], target.at[:, x], sems.at[which, x])

    for x in range(3):
        fetch(x, 0).start()
    fetch(1, 1).start()
    stencil_setup(high, low)
    for copy in small:
        copy.wait()

    zero = jnp.zeros((BLOCK, BLOCK), BF16)
    h, l = split(precond[...])
    given[0:BLOCK, :] = jnp.concatenate([h, l], axis=1)
    given[BLOCK:, :] = jnp.concatenate([h, zero], axis=1)
    right = jnp.concatenate([jnp.concatenate([h, l], axis=1)] * 2, axis=0)
    stacked = jnp.concatenate([faces[...].reshape(6 * BLOCK, BLOCK), OMEGA * block_matrix[...], coupling[...]], axis=0)
    h, l = split(folded(both(stacked), right))
    for d in range(4):
        rows = slice(d * BLOCK, (d + 1) * BLOCK)
        lateral[rows, :] = jnp.concatenate([h[rows], l[rows]], axis=1)
        lateral[(d + 4) * BLOCK : (d + 5) * BLOCK, :] = jnp.concatenate([h[rows], zero], axis=1)
    parts = [slice(d * BLOCK, (d + 1) * BLOCK) for d in (6, 4, 5)]
    central[0:BLOCK, :] = jnp.concatenate([h[rows] for rows in parts] + [l[rows] for rows in parts], axis=1)
    central[BLOCK:, :] = jnp.concatenate([h[rows] for rows in parts] + [zero] * 3, axis=1)
    h, l = h[7 * BLOCK :], l[7 * BLOCK :]
    none = jnp.zeros((SPACE, 2 * BLOCK), BF16)
    carry[...] = jnp.concatenate(
        [jnp.concatenate([h, l], axis=1), none, jnp.concatenate([h, zero[:SPACE]], axis=1), none], axis=0
    )

    def enter(x):
        fetch(x, 0).wait()
        position = lax.broadcasted_iota(jnp.int32, (NTD, LAYER, BLOCK), 1) + x * LAYER
        value = jnp.where(position < info[0], adjoint[:, x], 0.0)
        adjoint[:, x] = value
        stencil_split(x, value, high, low)

    enter(0)
    enter(1)
    later = {x: [(x + 2, 0), (x + 1, 1)] for x in layers(INNER)}
    later[2] += [(0, 1)]
    later[3] += [(EX - 1, 1)]
    for x in layers(INNER):
        for piece in later[x]:
            fetch(*piece).start()
        enter(x + 1)
        fetch(x, 1).wait()
        predict(x, field, adjoint, loads, relaxed, high, low, lateral, central, given, conductance)
    enter(EX - 1)
    for x in layers(OUTER):
        fetch(x, 1).wait()


def first_prediction(info, initial, forcing, conductance, block_matrix, precond, faces, coupling):
    return pl.pallas_call(
        first_kernel,
        out_shape=[VMEM(STACK, F32)] * 4
        + [VMEM(PADDED, BF16)] * 2
        + [VMEM(LATERAL, BF16), VMEM(CENTRAL, BF16), VMEM(SQUARE, BF16), VMEM(SQUARE, BF16)],
        in_specs=[INS, INH, INH, INV] + [INH] * 4,
        out_specs=[INV] * 10,
        scratch_shapes=[
            pltpu.VMEM((BLOCK, BLOCK), F32),
            pltpu.VMEM((BLOCK, BLOCK), F32),
            pltpu.VMEM((6, BLOCK, BLOCK), F32),
            pltpu.VMEM((SPACE, BLOCK), F32),
            pltpu.SemaphoreType.DMA((2, EX)),
            pltpu.SemaphoreType.DMA((4,)),
        ],
        compiler_params=params(16),
        cost_estimate=cost(0.01),
        name="first_inner",
    )(info, initial, forcing, conductance, block_matrix, precond, faces, coupling)


def next_kernel(adjoint, loads, relaxed, lateral, central, field, high, low):
    stencil_setup(high, low)
    for x in range(2):
        stencil_split(x, adjoint[:, x], high, low)
    for x in layers(INNER):
        stencil_split(x + 1, adjoint[:, x + 1], high, low)
        predict(x, field, adjoint, loads, relaxed, high, low, lateral, central)
    stencil_split(EX - 1, adjoint[:, EX - 1], high, low)


def next_prediction(adjoint, loads, relaxed, lateral, central):
    return pl.pallas_call(
        next_kernel,
        out_shape=[VMEM(STACK, F32), VMEM(PADDED, BF16), VMEM(PADDED, BF16)],
        in_specs=[INV] * 5,
        out_specs=[INV] * 3,
        compiler_params=params(16),
        cost_estimate=cost(0.01),
        name="next_inner",
    )(adjoint, loads, relaxed, lateral, central)


def rows_of(stack, t, runs):
    return jnp.concatenate([stack[t, first : first + count].reshape(count * LAYER, BLOCK) for first, count in runs], axis=0)


def chain(info, field, relaxed, carry, runs, trace, done=None):
    keep = jnp.concatenate(
        [
            (lax.broadcasted_iota(jnp.int32, (count * LAYER, BLOCK), 0) + first * LAYER < info[0]).astype(F32)
            for first, count in runs
        ],
        axis=0,
    ) > 0.5
    for t in reversed(range(NTD)):
        value = rows_of(field, t, runs)
        if trace is not None:
            value = value - rows_of(relaxed, t, runs) * folded(both(trace), carry[...])
        trace = jnp.where(keep, value, 0.0)
        at = 0
        for first, count in runs:
            rows = count * LAYER
            field[t, first : first + count] = trace[at : at + rows].reshape(count, LAYER, BLOCK)
            at += rows
        if done is not None:
            done(t)
    return trace


def packed(trace):
    half = trace.shape[0] // 2
    lane = lax.broadcasted_iota(jnp.int32, (half, BLOCK), 1)
    return jnp.where(lane < SPACE, trace[:half], pltpu.roll(trace[half:], SPACE, 1))


def unpacked(value):
    return jnp.concatenate([value, pltpu.roll(value, SPACE, 1)], axis=0)


def trace_shape(runs):
    return VMEM((len(layers(runs)) * LAYER // 2, BLOCK), F32)


def early_chain(info, field, relaxed, carry, runs, trace):
    @pl.when(info[1] == 1)
    def _():
        trace[...] = packed(chain(info, field, relaxed, carry, runs, None))


def face_matrix(lateral, d):
    top, bottom = pl.multiple_of(d * BLOCK, BLOCK), pl.multiple_of((d + 4) * BLOCK, BLOCK)
    return jnp.concatenate([lateral[pl.ds(top, BLOCK), :], lateral[pl.ds(bottom, BLOCK), :]], axis=0)


def inner_kernel(info, pred, relaxed, lateral, carry, y_near, y_far, field, trace):
    ((first, count),) = INNER
    for halo, at in ((y_near, near(info, 1)), (y_far, far(info, 1))):
        matrix = face_matrix(lateral, 2 + (at > 0).astype(jnp.int32))
        values = halo[:, first : first + count].reshape(NTD * count * EZ, BLOCK)
        term = folded(both(values), matrix).reshape(NTD, count, EZ, BLOCK)
        area = (slice(None), pl.ds(first, count), pl.ds(at, EZ))
        field[area] = field[area] - relaxed[area] * term
    early_chain(info, field, relaxed, carry, INNER, trace)


def inner_halos(info, field, relaxed, lateral, carry, y_halos):
    return pl.pallas_call(
        inner_kernel,
        out_shape=[VMEM(STACK, F32), trace_shape(INNER)],
        in_specs=[INS] + [INV] * 6,
        out_specs=[INV, INV],
        input_output_aliases={1: 0},
        compiler_params=params(8),
        cost_estimate=cost(2),
        name="inner_halos",
    )(info, field, relaxed, lateral, carry, *y_halos)


def outer_kernel(first_sweep, info, *refs):
    if first_sweep:
        conductance, given, *refs = refs
        (_, _, _, _, _, adjoint, lateral, central, carry, x_near, x_far, y_near, y_far,
         field, high, low, loads, relaxed, trace) = refs
    else:
        conductance = given = None
        (_, _, _, adjoint, lateral, central, carry, x_near, x_far, y_near, y_far, loads, relaxed,
         field, high, low, trace) = refs
    for halo, x in ((x_near, near(info, 0)), (x_far, far(info, 0))):
        h, l = split(halo[...])
        place = jnp.where(x > 0, EX + 1, 0)
        high[place, :, pl.ds(EZ, LAYER)] = h
        low[place, :, pl.ds(EZ, LAYER)] = l
    for halo, y in ((y_near, near(info, 1)), (y_far, far(info, 1))):
        place = pl.multiple_of(jnp.where(y > 0, LAYER + EZ, 0), EZ)
        for x in layers(OUTER):
            h, l = split(halo[:, x])
            high[x + 1, :, pl.ds(place, EZ)] = h
            low[x + 1, :, pl.ds(place, EZ)] = l
    for x in layers(OUTER):
        predict(x, field, adjoint, loads, relaxed, high, low, lateral, central, given, conductance)
    early_chain(info, field, relaxed, carry, OUTER, trace)


def outer_prediction(info, field, high, low, adjoint, lateral, central, carry, halos, loads, relaxed, given, conductance):
    first_sweep = given is not None
    if first_sweep:
        args = [info, conductance, given, field, high, low, loads, relaxed, adjoint, lateral, central, carry, *halos]
        outs = [VMEM(STACK, F32), VMEM(PADDED, BF16), VMEM(PADDED, BF16), VMEM(STACK, F32), VMEM(STACK, F32)]
        aliases = {k + 3: k for k in range(5)}
    else:
        args = [info, field, high, low, adjoint, lateral, central, carry, *halos, loads, relaxed]
        outs = [VMEM(STACK, F32), VMEM(PADDED, BF16), VMEM(PADDED, BF16)]
        aliases = {k + 1: k for k in range(3)}
    outs = outs + [trace_shape(OUTER)]
    out = pl.pallas_call(
        functools.partial(outer_kernel, first_sweep),
        out_shape=outs,
        in_specs=[INS] + [INV] * (len(args) - 1),
        out_specs=[INV] * len(outs),
        input_output_aliases=aliases,
        compiler_params=params(16),
        cost_estimate=cost(7),
        name="first_outer" if first_sweep else "next_outer",
    )(*args)
    if first_sweep:
        loads, relaxed = out[3:5]
    return out[0], out[-1], loads, relaxed


def late_chain(info, field, relaxed, carry, trace, runs):
    @pl.when(info[1] == 0)
    def _():
        chain(info, field, relaxed, carry, runs, unpacked(trace[...]))


def late_inner_kernel(info, field, relaxed, carry, trace, out):
    late_chain(info, out, relaxed, carry, trace, INNER)


def late_outer_kernel(info, field, relaxed, carry, trace, out, x_near, x_far, y_near, y_far):
    late_chain(info, out, relaxed, carry, trace, OUTER)
    x_near[...] = out[:, near(info, 0)]
    x_far[...] = out[:, far(info, 0)]
    y_near[...] = out[:, :, pl.ds(near(info, 1), EZ)]
    y_far[...] = out[:, :, pl.ds(far(info, 1), EZ)]


def after_trace(info, field, relaxed, carry, trace, inner):
    outs = [VMEM(STACK, F32)] + ([] if inner else FACES)
    return pl.pallas_call(
        late_inner_kernel if inner else late_outer_kernel,
        out_shape=outs,
        in_specs=[INS] + [INV] * 4,
        out_specs=[INV] * len(outs),
        input_output_aliases={1: 0},
        compiler_params=params(8),
        cost_estimate=cost(2),
        name="late_inner" if inner else "late_outer",
    )(info, field, relaxed, carry, trace)


def last_chain(info, relaxed, carry, trace, kept, out, sems, runs):
    copies = [
        [
            pltpu.make_async_copy(kept.at[t, pl.ds(first, count)], out.at[t, pl.ds(first, count)], sems.at[t, k])
            for k, (first, count) in enumerate(runs)
        ]
        for t in range(NTD)
    ]

    def send(t):
        for copy in copies[t]:
            copy.start()

    @pl.when(info[1] == 0)
    def _():
        chain(info, kept, relaxed, carry, runs, unpacked(trace[...]), send)

    @pl.when(info[1] == 1)
    def _():
        for t in range(NTD):
            send(t)

    for t in range(NTD):
        for copy in copies[t]:
            copy.wait()


def last_inner_kernel(info, field, relaxed, carry, trace, kept, out, sems):
    last_chain(info, relaxed, carry, trace, kept, out, sems, INNER)


def last_outer_kernel(info, field, relaxed, carry, trace, given, kept, out, sems):
    last_chain(info, relaxed, carry, trace, kept, out, sems, OUTER)


def last(info, field, relaxed, carry, trace, given):
    inner = given is None
    args = [info, field, relaxed, carry, trace] + ([] if inner else [given])
    return pl.pallas_call(
        last_inner_kernel if inner else last_outer_kernel,
        out_shape=[VMEM(STACK, F32), pltpu.HBM(STACK, F32)],
        in_specs=[INS] + [INV] * 4 + ([] if inner else [INH]),
        out_specs=[INV, INH],
        input_output_aliases={1: 0} if inner else {1: 0, 5: 1},
        scratch_shapes=[pltpu.SemaphoreType.DMA((NTD, 2))],
        compiler_params=params(8),
        cost_estimate=cost(3),
        name="last_inner" if inner else "last_outer",
    )(*args)


def exchanged(value, axis, first):
    count = lax.axis_size(axis)
    pairs = [(i, i + 1) for i in range(first, count - 1, 2)]
    return lax.ppermute(value, axis, pairs + [(j, i) for i, j in pairs])


def sent_back(value):
    return lax.ppermute(value, "tm", [(1, 0)])


def body(forcing, initial, conductance, counts, block_matrix, precond, face_coupling, time_coupling):
    shape = forcing.shape
    in_hbm = functools.partial(pltpu.with_memory_space_constraint, memory_space=pltpu.HBM)
    forcing, initial = in_hbm(forcing.reshape(STACK)), in_hbm(initial.reshape(STACK))
    block_matrix, precond, face_coupling, time_coupling = map(
        in_hbm, (block_matrix, precond, face_coupling, time_coupling)
    )
    even_x = 1 - lax.rem(lax.axis_index("sx"), 2).astype(jnp.int32)
    even_y = 1 - lax.rem(lax.axis_index("sy"), 2).astype(jnp.int32)
    info = jnp.stack(
        [counts[0, 0], lax.axis_index("tm").astype(jnp.int32), even_x * (EX - 1), even_y * (LAYER - EZ)]
    )

    def halos_of(x_near, x_far, y_near, y_far):
        return (
            exchanged(x_near, "sx", 0), exchanged(x_far, "sx", 1),
            exchanged(y_near, "sy", 0), exchanged(y_far, "sy", 1),
        )

    halos = halos_of(*faces_of_initial(info, initial))
    field, adjoint, loads, relaxed, high, low, lateral, central, carry, given = first_prediction(
        info, initial, forcing, conductance, block_matrix, precond, face_coupling, time_coupling
    )
    for sweep in range(SWEEPS):
        if sweep:
            adjoint, given = field, None
            field, high, low = next_prediction(adjoint, loads, relaxed, lateral, central)
        field, inner = inner_halos(info, field, relaxed, lateral, carry, halos[2:])
        inner = sent_back(inner)
        field, outer, loads, relaxed = outer_prediction(
            info, field, high, low, adjoint, lateral, central, carry, halos, loads, relaxed, given, conductance
        )
        outer = sent_back(outer)
        if sweep < SWEEPS - 1:
            (field,) = after_trace(info, field, relaxed, carry, inner, True)
            field, *faces = after_trace(info, field, relaxed, carry, outer, False)
            halos = halos_of(*faces)
        else:
            field, out = last(info, field, relaxed, carry, inner, None)
            field, out = last(info, field, relaxed, carry, outer, out)
    return out.reshape(shape)


def solution(mesh):
    in_specs = (
        P("tm", "sx", "sy", None, None),
        P("tm", "sx", "sy", None, None),
        P("tm", "sx", "sy", None),
        P("sx", "sy"),
        P(),
        P(),
        P(),
        P(),
    )
    out_specs = P("tm", "sx", "sy", None, None)
    return jax.shard_map(body, mesh=mesh, in_specs=in_specs, out_specs=out_specs, check_vma=False)
```

```python
import functools

import jax
import jax.numpy as jnp
from jax import lax
from jax.experimental import pallas as pl
from jax.experimental.pallas import tpu as pltpu
from jax.sharding import PartitionSpec as P

SWEEPS = 2
OMEGA = 0.7
NTD, EX, EY, EZ, BLOCK = 4, 8, 16, 16, 128
SPACE = BLOCK // 2
LAYER = EY * EZ
F32, BF16 = jnp.float32, jnp.bfloat16
VMEM = pltpu.VMEM
ANY = pl.BlockSpec(memory_space=pl.ANY)
INH = pl.BlockSpec(memory_space=pltpu.HBM)
INV = pl.BlockSpec(memory_space=VMEM)
INS = pl.BlockSpec(memory_space=pltpu.SMEM)
INNER = ((1, 5),)
OUTER = ((0, 1), (6, 2))


def params(mib):
    return pltpu.CompilerParams(vmem_limit_bytes=mib << 20)


def cost(us):
    return pl.CostEstimate(flops=int(us * 1.0e9), bytes_accessed=0, transcendentals=0)


def split(value):
    high = value.astype(BF16)
    low = (value - high.astype(F32)).astype(BF16)
    return high, low


def dot(rows, matrix):
    return jnp.dot(rows, matrix, preferred_element_type=F32)


def both(value):
    return jnp.concatenate(split(value), axis=-1)


def folded(rows, matrix):
    out = dot(rows, matrix)
    return out[:, :BLOCK] + out[:, BLOCK:]


def mask(info, first, rows):
    position = lax.broadcasted_iota(jnp.int32, (rows, BLOCK), 0) + first * LAYER
    return position < info[0]


def near(info, dim):
    return pl.multiple_of(info[3], EZ) if dim else info[2]


def far(info, dim):
    return pl.multiple_of(LAYER - EZ - info[3], EZ) if dim else EX - 1 - info[2]


def faces_kernel(info, initial, x_near, x_far, y_near, y_far, sems):
    places = (near(info, 0), far(info, 0), near(info, 1), far(info, 1))
    refs = (x_near, x_far, y_near, y_far)
    copies = [
        pltpu.make_async_copy(initial.at[:, at] if k < 2 else initial.at[:, :, pl.ds(at, EZ)], ref, sems.at[k])
        for k, (ref, at) in enumerate(zip(refs, places))
    ]
    for copy in copies:
        copy.start()
    for copy, ref, at in zip(copies[:2], refs[:2], places[:2]):
        copy.wait()
        keep = mask(info, at, LAYER)
        for t in range(NTD):
            ref[t] = jnp.where(keep, ref[t], 0.0)
    for copy, ref, at in zip(copies[2:], refs[2:], places[2:]):
        copy.wait()
        for x in range(EX):
            position = lax.broadcasted_iota(jnp.int32, (EZ, BLOCK), 0) + (x * LAYER + at)
            for t in range(NTD):
                ref[t, x] = jnp.where(position < info[0], ref[t, x], 0.0)


FACES = [VMEM((NTD, LAYER, BLOCK), F32)] * 2 + [VMEM((NTD, EX, EZ, BLOCK), F32)] * 2


def faces_of_initial(info, initial):
    return pl.pallas_call(
        faces_kernel,
        out_shape=FACES,
        in_specs=[INS, INH],
        out_specs=[INV] * 4,
        scratch_shapes=[pltpu.SemaphoreType.DMA((4,))],
        compiler_params=params(4),
        cost_estimate=cost(2),
        name="faces",
    )(info, initial)


def stencil_setup(high, low):
    for ref in (high, low):
        for x in (0, EX + 1):
            ref[x] = jnp.zeros(ref.shape[1:], BF16)
        for x in range(1, EX + 1):
            for t in range(NTD):
                ref[x, t, 0:EZ] = jnp.zeros((EZ, BLOCK), BF16)
                ref[x, t, EZ + LAYER :] = jnp.zeros((EZ, BLOCK), BF16)


def stencil_split(x, value, high, low):
    h, l = split(value)
    high[x + 1, :, pl.ds(EZ, LAYER)] = h
    low[x + 1, :, pl.ds(EZ, LAYER)] = l


def flat(value):
    return value.reshape(NTD * LAYER, BLOCK)


def stencil_layer(x, adjoint, high, low, lateral, central):
    pieces = []
    for ref in (high, low):
        pieces += [
            flat(ref[x, :, pl.ds(EZ, LAYER)]),
            flat(ref[x + 2, :, pl.ds(EZ, LAYER)]),
            flat(ref[x + 1, :, pl.ds(0, LAYER)]),
            flat(ref[x + 1, :, pl.ds(2 * EZ, LAYER)]),
        ]
    around = folded(jnp.concatenate(pieces, axis=1), lateral[...])
    own = [flat(ref[x + 1, :, pl.ds(EZ, LAYER)]) for ref in (high, low)]
    out = dot(jnp.concatenate(own, axis=1), central[...])
    own, below, above = (
        out[:, k * BLOCK : (k + 1) * BLOCK] + out[:, (k + 3) * BLOCK : (k + 4) * BLOCK] for k in range(3)
    )
    depth = lax.broadcasted_iota(jnp.int32, (NTD * LAYER, BLOCK), 0) % EZ
    below = jnp.where(depth == 0, 0.0, pltpu.roll(below, 1, 0))
    above = jnp.where(depth == EZ - 1, 0.0, pltpu.roll(above, NTD * LAYER - 1, 0))
    return adjoint - own, around + below + above


STACK = (NTD, EX, LAYER, BLOCK)
PADDED = (EX + 2, NTD, LAYER + 2 * EZ, BLOCK)
LATERAL = (8 * BLOCK, 2 * BLOCK)
CENTRAL = (2 * BLOCK, 6 * BLOCK)
SQUARE = (2 * BLOCK, 2 * BLOCK)


def layers(runs):
    return [x for first, count in runs for x in range(first, first + count)]


def row_factors(conductance, x, relaxed):
    factor = []
    for t in range(NTD):
        inverse = OMEGA / conductance[t, x]
        spread = jnp.broadcast_to(inverse[:, None, :], (EY, EZ, EZ)).reshape(LAYER, EZ)
        lane = lax.broadcasted_iota(jnp.int32, (LAYER, EZ), 1)
        depth = lax.broadcasted_iota(jnp.int32, (LAYER, EZ), 0) % EZ
        column = jnp.sum(jnp.where(lane == depth, spread, 0.0), axis=1, keepdims=True)
        column = jnp.broadcast_to(column, (LAYER, BLOCK))
        relaxed[t, x] = column
        factor.append(column)
    return jnp.concatenate(factor, axis=0)


def predict(x, field, adjoint, loads, relaxed, high, low, lateral, central, given=None, conductance=None):
    if given is None:
        factor, rest = flat(relaxed[:, x]), flat(loads[:, x])
    else:
        factor = row_factors(conductance, x, relaxed)
        rest = factor * folded(both(flat(loads[:, x])), given[...])
        loads[:, x] = rest.reshape(NTD, LAYER, BLOCK)
    own, around = stencil_layer(x, flat(adjoint[:, x]), high, low, lateral, central)
    field[:, x] = (own + rest - factor * around).reshape(NTD, LAYER, BLOCK)


def first_kernel(
    info, initial, forcing, conductance, block_matrix_hbm, precond_hbm, faces_hbm, coupling_hbm,
    field, adjoint, loads, relaxed, high, low, lateral, central, carry, given,
    block_matrix, precond, faces, coupling, sems, small_sems,
):
    small = [
        pltpu.make_async_copy(source, target, small_sems.at[k])
        for k, (source, target) in enumerate(
            [(precond_hbm, precond), (faces_hbm, faces), (block_matrix_hbm, block_matrix), (coupling_hbm, coupling)]
        )
    ]
    for copy in small:
        copy.start()

    def fetch(x, which):
        source, target = ((initial, adjoint), (forcing, loads))[which]
        return pltpu.make_async_copy(source.at[:, x], target.at[:, x], sems.at[which, x])

    for x in range(3):
        fetch(x, 0).start()
    fetch(1, 1).start()
    stencil_setup(high, low)
    for copy in small:
        copy.wait()

    zero = jnp.zeros((BLOCK, BLOCK), BF16)
    h, l = split(precond[...])
    given[0:BLOCK, :] = jnp.concatenate([h, l], axis=1)
    given[BLOCK:, :] = jnp.concatenate([h, zero], axis=1)
    right = jnp.concatenate([jnp.concatenate([h, l], axis=1)] * 2, axis=0)
    stacked = jnp.concatenate([faces[...].reshape(6 * BLOCK, BLOCK), OMEGA * block_matrix[...], coupling[...]], axis=0)
    h, l = split(folded(both(stacked), right))
    for d in range(4):
        rows = slice(d * BLOCK, (d + 1) * BLOCK)
        lateral[rows, :] = jnp.concatenate([h[rows], l[rows]], axis=1)
        lateral[(d + 4) * BLOCK : (d + 5) * BLOCK, :] = jnp.concatenate([h[rows], zero], axis=1)
    parts = [slice(d * BLOCK, (d + 1) * BLOCK) for d in (6, 4, 5)]
    central[0:BLOCK, :] = jnp.concatenate([h[rows] for rows in parts] + [l[rows] for rows in parts], axis=1)
    central[BLOCK:, :] = jnp.concatenate([h[rows] for rows in parts] + [zero] * 3, axis=1)
    h, l = h[7 * BLOCK :], l[7 * BLOCK :]
    none = jnp.zeros((SPACE, 2 * BLOCK), BF16)
    carry[...] = jnp.concatenate(
        [jnp.concatenate([h, l], axis=1), none, jnp.concatenate([h, zero[:SPACE]], axis=1), none], axis=0
    )

    def enter(x):
        fetch(x, 0).wait()
        position = lax.broadcasted_iota(jnp.int32, (NTD, LAYER, BLOCK), 1) + x * LAYER
        value = jnp.where(position < info[0], adjoint[:, x], 0.0)
        adjoint[:, x] = value
        stencil_split(x, value, high, low)

    enter(0)
    enter(1)
    later = {x: [(x + 2, 0), (x + 1, 1)] for x in layers(INNER)}
    later[2] += [(0, 1)]
    later[3] += [(EX - 1, 1)]
    for x in layers(INNER):
        for piece in later[x]:
            fetch(*piece).start()
        enter(x + 1)
        fetch(x, 1).wait()
        predict(x, field, adjoint, loads, relaxed, high, low, lateral, central, given, conductance)
    enter(EX - 1)
    for x in layers(OUTER):
        fetch(x, 1).wait()


def first_prediction(info, initial, forcing, conductance, block_matrix, precond, faces, coupling):
    return pl.pallas_call(
        first_kernel,
        out_shape=[VMEM(STACK, F32)] * 4
        + [VMEM(PADDED, BF16)] * 2
        + [VMEM(LATERAL, BF16), VMEM(CENTRAL, BF16), VMEM(SQUARE, BF16), VMEM(SQUARE, BF16)],
        in_specs=[INS, INH, INH, INV] + [INH] * 4,
        out_specs=[INV] * 10,
        scratch_shapes=[
            pltpu.VMEM((BLOCK, BLOCK), F32),
            pltpu.VMEM((BLOCK, BLOCK), F32),
            pltpu.VMEM((6, BLOCK, BLOCK), F32),
            pltpu.VMEM((SPACE, BLOCK), F32),
            pltpu.SemaphoreType.DMA((2, EX)),
            pltpu.SemaphoreType.DMA((4,)),
        ],
        compiler_params=params(16),
        cost_estimate=cost(0.01),
        name="first_inner",
    )(info, initial, forcing, conductance, block_matrix, precond, faces, coupling)


def next_kernel(adjoint, loads, relaxed, lateral, central, field, high, low):
    stencil_setup(high, low)
    for x in range(2):
        stencil_split(x, adjoint[:, x], high, low)
    for x in layers(INNER):
        stencil_split(x + 1, adjoint[:, x + 1], high, low)
        predict(x, field, adjoint, loads, relaxed, high, low, lateral, central)
    stencil_split(EX - 1, adjoint[:, EX - 1], high, low)


def next_prediction(adjoint, loads, relaxed, lateral, central):
    return pl.pallas_call(
        next_kernel,
        out_shape=[VMEM(STACK, F32), VMEM(PADDED, BF16), VMEM(PADDED, BF16)],
        in_specs=[INV] * 5,
        out_specs=[INV] * 3,
        compiler_params=params(16),
        cost_estimate=cost(0.01),
        name="next_inner",
    )(adjoint, loads, relaxed, lateral, central)


def rows_of(stack, t, runs):
    return jnp.concatenate([stack[t, first : first + count].reshape(count * LAYER, BLOCK) for first, count in runs], axis=0)


def chain(info, field, relaxed, carry, runs, trace, done=None):
    keep = jnp.concatenate(
        [
            (lax.broadcasted_iota(jnp.int32, (count * LAYER, BLOCK), 0) + first * LAYER < info[0]).astype(F32)
            for first, count in runs
        ],
        axis=0,
    ) > 0.5
    for t in reversed(range(NTD)):
        value = rows_of(field, t, runs)
        if trace is not None:
            value = value - rows_of(relaxed, t, runs) * folded(both(trace), carry[...])
        trace = jnp.where(keep, value, 0.0)
        at = 0
        for first, count in runs:
            rows = count * LAYER
            field[t, first : first + count] = trace[at : at + rows].reshape(count, LAYER, BLOCK)
            at += rows
        if done is not None:
            done(t)
    return trace


def packed(trace):
    half = trace.shape[0] // 2
    lane = lax.broadcasted_iota(jnp.int32, (half, BLOCK), 1)
    return jnp.where(lane < SPACE, trace[:half], pltpu.roll(trace[half:], SPACE, 1))


def unpacked(value):
    return jnp.concatenate([value, pltpu.roll(value, SPACE, 1)], axis=0)


def trace_shape(runs):
    return VMEM((len(layers(runs)) * LAYER // 2, BLOCK), F32)


def early_chain(info, field, relaxed, carry, runs, trace):
    @pl.when(info[1] == 1)
    def _():
        trace[...] = packed(chain(info, field, relaxed, carry, runs, None))

    @pl.when(info[1] == 0)
    def _():
        trace[...] = jnp.zeros(trace.shape, F32)


def face_matrix(lateral, d):
    top, bottom = pl.multiple_of(d * BLOCK, BLOCK), pl.multiple_of((d + 4) * BLOCK, BLOCK)
    return jnp.concatenate([lateral[pl.ds(top, BLOCK), :], lateral[pl.ds(bottom, BLOCK), :]], axis=0)


def inner_kernel(info, pred, relaxed, lateral, carry, y_near, y_far, field, trace):
    ((first, count),) = INNER
    for halo, at, has in ((y_near, near(info, 1), 1), (y_far, far(info, 1), info[5])):
        matrix = face_matrix(lateral, 2 + (at > 0).astype(jnp.int32))
        values = jnp.where(has > 0, halo[:, first : first + count].reshape(NTD * count * EZ, BLOCK), 0.0)
        term = folded(both(values), matrix).reshape(NTD, count, EZ, BLOCK)
        area = (slice(None), pl.ds(first, count), pl.ds(at, EZ))
        field[area] = field[area] - relaxed[area] * term
    early_chain(info, field, relaxed, carry, INNER, trace)


def inner_halos(info, field, relaxed, lateral, carry, y_halos):
    return pl.pallas_call(
        inner_kernel,
        out_shape=[VMEM(STACK, F32), trace_shape(INNER)],
        in_specs=[INS] + [INV] * 6,
        out_specs=[INV, INV],
        input_output_aliases={1: 0},
        compiler_params=params(8),
        cost_estimate=cost(2),
        name="inner_halos",
    )(info, field, relaxed, lateral, carry, *y_halos)


def outer_kernel(first_sweep, info, *refs):
    if first_sweep:
        conductance, given, *refs = refs
        (_, _, _, _, _, adjoint, lateral, central, carry, x_near, x_far, y_near, y_far,
         field, high, low, loads, relaxed, trace) = refs
    else:
        conductance = given = None
        (_, _, _, adjoint, lateral, central, carry, x_near, x_far, y_near, y_far, loads, relaxed,
         field, high, low, trace) = refs
    for halo, x, has in ((x_near, near(info, 0), 1), (x_far, far(info, 0), info[4])):
        h, l = split(jnp.where(has > 0, halo[...], 0.0))
        place = jnp.where(x > 0, EX + 1, 0)
        high[place, :, pl.ds(EZ, LAYER)] = h
        low[place, :, pl.ds(EZ, LAYER)] = l
    for halo, y, has in ((y_near, near(info, 1), 1), (y_far, far(info, 1), info[5])):
        place = pl.multiple_of(jnp.where(y > 0, LAYER + EZ, 0), EZ)
        for x in layers(OUTER):
            h, l = split(jnp.where(has > 0, halo[:, x], 0.0))
            high[x + 1, :, pl.ds(place, EZ)] = h
            low[x + 1, :, pl.ds(place, EZ)] = l
    for x in layers(OUTER):
        predict(x, field, adjoint, loads, relaxed, high, low, lateral, central, given, conductance)
    early_chain(info, field, relaxed, carry, OUTER, trace)


def outer_prediction(info, field, high, low, adjoint, lateral, central, carry, halos, loads, relaxed, given, conductance):
    first_sweep = given is not None
    if first_sweep:
        args = [info, conductance, given, field, high, low, loads, relaxed, adjoint, lateral, central, carry, *halos]
        outs = [VMEM(STACK, F32), VMEM(PADDED, BF16), VMEM(PADDED, BF16), VMEM(STACK, F32), VMEM(STACK, F32)]
        aliases = {k + 3: k for k in range(5)}
    else:
        args = [info, field, high, low, adjoint, lateral, central, carry, *halos, loads, relaxed]
        outs = [VMEM(STACK, F32), VMEM(PADDED, BF16), VMEM(PADDED, BF16)]
        aliases = {k + 1: k for k in range(3)}
    outs = outs + [trace_shape(OUTER)]
    out = pl.pallas_call(
        functools.partial(outer_kernel, first_sweep),
        out_shape=outs,
        in_specs=[INS] + [INV] * (len(args) - 1),
        out_specs=[INV] * len(outs),
        input_output_aliases=aliases,
        compiler_params=params(16),
        cost_estimate=cost(7),
        name="first_outer" if first_sweep else "next_outer",
    )(*args)
    if first_sweep:
        loads, relaxed = out[3:5]
    return out[0], out[-1], loads, relaxed


def late_chain(info, field, relaxed, carry, trace, runs):
    @pl.when(info[1] == 0)
    def _():
        chain(info, field, relaxed, carry, runs, unpacked(trace[...]))


def late_inner_kernel(info, field, relaxed, carry, trace, out):
    late_chain(info, out, relaxed, carry, trace, INNER)


def late_outer_kernel(info, field, relaxed, carry, trace, out, x_near, x_far, y_near, y_far):
    late_chain(info, out, relaxed, carry, trace, OUTER)
    x_near[...] = out[:, near(info, 0)]
    x_far[...] = out[:, far(info, 0)]
    y_near[...] = out[:, :, pl.ds(near(info, 1), EZ)]
    y_far[...] = out[:, :, pl.ds(far(info, 1), EZ)]


def after_trace(info, field, relaxed, carry, trace, inner):
    outs = [VMEM(STACK, F32)] + ([] if inner else FACES)
    return pl.pallas_call(
        late_inner_kernel if inner else late_outer_kernel,
        out_shape=outs,
        in_specs=[INS] + [INV] * 4,
        out_specs=[INV] * len(outs),
        input_output_aliases={1: 0},
        compiler_params=params(8),
        cost_estimate=cost(2),
        name="late_inner" if inner else "late_outer",
    )(info, field, relaxed, carry, trace)


def last_chain(info, relaxed, carry, trace, kept, out, sems, runs):
    copies = [
        [
            pltpu.make_async_copy(kept.at[t, pl.ds(first, count)], out.at[t, pl.ds(first, count)], sems.at[t, k])
            for k, (first, count) in enumerate(runs)
        ]
        for t in range(NTD)
    ]

    def send(t):
        for copy in copies[t]:
            copy.start()

    @pl.when(info[1] == 0)
    def _():
        chain(info, kept, relaxed, carry, runs, unpacked(trace[...]), send)

    @pl.when(info[1] == 1)
    def _():
        for t in range(NTD):
            send(t)

    for t in range(NTD):
        for copy in copies[t]:
            copy.wait()


def last_inner_kernel(info, field, relaxed, carry, trace, kept, out, sems):
    last_chain(info, relaxed, carry, trace, kept, out, sems, INNER)


def last_outer_kernel(info, field, relaxed, carry, trace, given, kept, out, sems):
    last_chain(info, relaxed, carry, trace, kept, out, sems, OUTER)


def last(info, field, relaxed, carry, trace, given):
    inner = given is None
    args = [info, field, relaxed, carry, trace] + ([] if inner else [given])
    return pl.pallas_call(
        last_inner_kernel if inner else last_outer_kernel,
        out_shape=[VMEM(STACK, F32), pltpu.HBM(STACK, F32)],
        in_specs=[INS] + [INV] * 4 + ([] if inner else [INH]),
        out_specs=[INV, INH],
        input_output_aliases={1: 0} if inner else {1: 0, 5: 1},
        scratch_shapes=[pltpu.SemaphoreType.DMA((NTD, 2))],
        compiler_params=params(8),
        cost_estimate=cost(3),
        name="last_inner" if inner else "last_outer",
    )(*args)


def both_ways(pairs):
    return pairs + [(j, i) for i, j in pairs]


def exchanged(value, axis, first):
    count = lax.axis_size(axis)
    return lax.ppermute(value, axis, both_ways([(i, (i + 1) % count) for i in range(first, count, 2)]))


def exchanged_far_x(value):
    count, lines = lax.axis_size("sx"), lax.axis_size("sy")
    pairs = [(i * lines + k, (i + 1) * lines + k) for i in range(1, count - 1, 2) for k in range(lines)]
    pairs += [(i * lines + k, i * lines + k + 1) for i in (0, count - 1) for k in range(0, lines, 2)]
    return lax.ppermute(value, ("sx", "sy"), both_ways(pairs))


def sent_back(value):
    return lax.ppermute(value, "tm", [(1, 0), (0, 1)])


def body(forcing, initial, conductance, counts, block_matrix, precond, face_coupling, time_coupling):
    shape = forcing.shape
    in_hbm = functools.partial(pltpu.with_memory_space_constraint, memory_space=pltpu.HBM)
    forcing, initial = in_hbm(forcing.reshape(STACK)), in_hbm(initial.reshape(STACK))
    block_matrix, precond, face_coupling, time_coupling = map(
        in_hbm, (block_matrix, precond, face_coupling, time_coupling)
    )
    even_x = 1 - lax.rem(lax.axis_index("sx"), 2).astype(jnp.int32)
    even_y = 1 - lax.rem(lax.axis_index("sy"), 2).astype(jnp.int32)
    at_x, at_y = lax.axis_index("sx"), lax.axis_index("sy")
    has_x = jnp.logical_and(at_x > 0, at_x < lax.axis_size("sx") - 1).astype(jnp.int32)
    has_y = jnp.logical_and(at_y > 0, at_y < lax.axis_size("sy") - 1).astype(jnp.int32)
    info = jnp.stack(
        [
            counts[0, 0], lax.axis_index("tm").astype(jnp.int32),
            even_x * (EX - 1), even_y * (LAYER - EZ), has_x, has_y,
        ]
    )

    def halos_of(x_near, x_far, y_near, y_far):
        return (
            exchanged(x_near, "sx", 0), exchanged_far_x(x_far),
            exchanged(y_near, "sy", 0), exchanged(y_far, "sy", 1),
        )

    halos = halos_of(*faces_of_initial(info, initial))
    field, adjoint, loads, relaxed, high, low, lateral, central, carry, given = first_prediction(
        info, initial, forcing, conductance, block_matrix, precond, face_coupling, time_coupling
    )
    for sweep in range(SWEEPS):
        if sweep:
            adjoint, given = field, None
            field, high, low = next_prediction(adjoint, loads, relaxed, lateral, central)
        field, inner = inner_halos(info, field, relaxed, lateral, carry, halos[2:])
        inner = sent_back(inner)
        field, outer, loads, relaxed = outer_prediction(
            info, field, high, low, adjoint, lateral, central, carry, halos, loads, relaxed, given, conductance
        )
        outer = sent_back(outer)
        if sweep < SWEEPS - 1:
            (field,) = after_trace(info, field, relaxed, carry, inner, True)
            field, *faces = after_trace(info, field, relaxed, carry, outer, False)
            halos = halos_of(*faces)
        else:
            field, out = last(info, field, relaxed, carry, inner, None)
            field, out = last(info, field, relaxed, carry, outer, out)
    return out.reshape(shape)


def solution(mesh):
    in_specs = (
        P("tm", "sx", "sy", None, None),
        P("tm", "sx", "sy", None, None),
        P("tm", "sx", "sy", None),
        P("sx", "sy"),
        P(),
        P(),
        P(),
        P(),
    )
    out_specs = P("tm", "sx", "sy", None, None)
    return jax.shard_map(body, mesh=mesh, in_specs=in_specs, out_specs=out_specs, check_vma=False)
```

```python
import functools

import jax
import jax.numpy as jnp
from jax import lax
from jax.experimental import pallas as pl
from jax.experimental.pallas import tpu as pltpu
from jax.sharding import PartitionSpec as P

SWEEPS = 2
OMEGA = 0.7
NTD, EX, EY, EZ, BLOCK = 4, 8, 16, 16, 128
SPACE = BLOCK // 2
LAYER = EY * EZ
F32, BF16 = jnp.float32, jnp.bfloat16
VMEM = pltpu.VMEM
ANY = pl.BlockSpec(memory_space=pl.ANY)
INH = pl.BlockSpec(memory_space=pltpu.HBM)
INV = pl.BlockSpec(memory_space=VMEM)
INS = pl.BlockSpec(memory_space=pltpu.SMEM)
INNER = ((1, 5),)
OUTER = ((0, 1), (6, 2))


def params(mib):
    return pltpu.CompilerParams(vmem_limit_bytes=mib << 20)


def cost(us):
    return pl.CostEstimate(flops=int(us * 1.0e9), bytes_accessed=0, transcendentals=0)


def split(value):
    high = value.astype(BF16)
    low = (value - high.astype(F32)).astype(BF16)
    return high, low


def dot(rows, matrix):
    return jnp.dot(rows, matrix, preferred_element_type=F32)


def both(value):
    return jnp.concatenate(split(value), axis=-1)


def folded(rows, matrix):
    out = dot(rows, matrix)
    return out[:, :BLOCK] + out[:, BLOCK:]


def mask(info, first, rows):
    position = lax.broadcasted_iota(jnp.int32, (rows, BLOCK), 0) + first * LAYER
    return position < info[0]


def near(info, dim):
    return pl.multiple_of(info[3], EZ) if dim else info[2]


def far(info, dim):
    return pl.multiple_of(LAYER - EZ - info[3], EZ) if dim else EX - 1 - info[2]


def faces_kernel(info, initial, x_near, x_far, y_near, y_far, sems):
    places = (near(info, 0), far(info, 0), near(info, 1), far(info, 1))
    refs = (x_near, x_far, y_near, y_far)
    copies = [
        pltpu.make_async_copy(initial.at[:, at] if k < 2 else initial.at[:, :, pl.ds(at, EZ)], ref, sems.at[k])
        for k, (ref, at) in enumerate(zip(refs, places))
    ]
    for copy in copies:
        copy.start()
    for copy, ref, at in zip(copies[:2], refs[:2], places[:2]):
        copy.wait()
        keep = mask(info, at, LAYER)
        for t in range(NTD):
            ref[t] = jnp.where(keep, ref[t], 0.0)
    for copy, ref, at in zip(copies[2:], refs[2:], places[2:]):
        copy.wait()
        for x in range(EX):
            position = lax.broadcasted_iota(jnp.int32, (EZ, BLOCK), 0) + (x * LAYER + at)
            for t in range(NTD):
                ref[t, x] = jnp.where(position < info[0], ref[t, x], 0.0)


FACES = [VMEM((NTD, LAYER, BLOCK), F32)] * 2 + [VMEM((NTD, EX, EZ, BLOCK), F32)] * 2


def faces_of_initial(info, initial):
    return pl.pallas_call(
        faces_kernel,
        out_shape=FACES,
        in_specs=[INS, INH],
        out_specs=[INV] * 4,
        scratch_shapes=[pltpu.SemaphoreType.DMA((4,))],
        compiler_params=params(4),
        cost_estimate=cost(2),
        name="faces",
    )(info, initial)


def stencil_setup(high, low):
    for ref in (high, low):
        for x in (0, EX + 1):
            ref[x] = jnp.zeros(ref.shape[1:], BF16)
        for x in range(1, EX + 1):
            for t in range(NTD):
                ref[x, t, 0:EZ] = jnp.zeros((EZ, BLOCK), BF16)
                ref[x, t, EZ + LAYER :] = jnp.zeros((EZ, BLOCK), BF16)


def stencil_split(x, value, high, low):
    h, l = split(value)
    high[x + 1, :, pl.ds(EZ, LAYER)] = h
    low[x + 1, :, pl.ds(EZ, LAYER)] = l


def flat(value):
    return value.reshape(NTD * LAYER, BLOCK)


def stencil_layer(x, adjoint, high, low, lateral, central):
    pieces = []
    for ref in (high, low):
        pieces += [
            flat(ref[x, :, pl.ds(EZ, LAYER)]),
            flat(ref[x + 2, :, pl.ds(EZ, LAYER)]),
            flat(ref[x + 1, :, pl.ds(0, LAYER)]),
            flat(ref[x + 1, :, pl.ds(2 * EZ, LAYER)]),
        ]
    around = folded(jnp.concatenate(pieces, axis=1), lateral[...])
    own = [flat(ref[x + 1, :, pl.ds(EZ, LAYER)]) for ref in (high, low)]
    out = dot(jnp.concatenate(own, axis=1), central[...])
    own, below, above = (
        out[:, k * BLOCK : (k + 1) * BLOCK] + out[:, (k + 3) * BLOCK : (k + 4) * BLOCK] for k in range(3)
    )
    depth = lax.broadcasted_iota(jnp.int32, (NTD * LAYER, BLOCK), 0) % EZ
    below = jnp.where(depth == 0, 0.0, pltpu.roll(below, 1, 0))
    above = jnp.where(depth == EZ - 1, 0.0, pltpu.roll(above, NTD * LAYER - 1, 0))
    return adjoint - own, around + below + above


STACK = (NTD, EX, LAYER, BLOCK)
PADDED = (EX + 2, NTD, LAYER + 2 * EZ, BLOCK)
LATERAL = (8 * BLOCK, 2 * BLOCK)
CENTRAL = (2 * BLOCK, 6 * BLOCK)
SQUARE = (2 * BLOCK, 2 * BLOCK)


def layers(runs):
    return [x for first, count in runs for x in range(first, first + count)]


def row_factors(conductance, x, relaxed):
    factor = []
    for t in range(NTD):
        inverse = OMEGA / conductance[t, x]
        spread = jnp.broadcast_to(inverse[:, None, :], (EY, EZ, EZ)).reshape(LAYER, EZ)
        lane = lax.broadcasted_iota(jnp.int32, (LAYER, EZ), 1)
        depth = lax.broadcasted_iota(jnp.int32, (LAYER, EZ), 0) % EZ
        column = jnp.sum(jnp.where(lane == depth, spread, 0.0), axis=1, keepdims=True)
        column = jnp.broadcast_to(column, (LAYER, BLOCK))
        relaxed[t, x] = column
        factor.append(column)
    return jnp.concatenate(factor, axis=0)


def predict(x, field, adjoint, loads, relaxed, high, low, lateral, central, given=None, conductance=None, forcing=None):
    if given is None:
        factor, rest = flat(relaxed[:, x]), flat(loads[:, x])
    else:
        factor = row_factors(conductance, x, relaxed)
        rest = factor * folded(both(flat(forcing[:, x])), given[...])
        loads[:, x] = rest.reshape(NTD, LAYER, BLOCK)
    own, around = stencil_layer(x, flat(adjoint[:, x]), high, low, lateral, central)
    field[:, x] = (own + rest - factor * around).reshape(NTD, LAYER, BLOCK)


def first_kernel(
    info, initial, forcing, conductance, block_matrix, precond, faces, coupling,
    field, adjoint, loads, relaxed, high, low, lateral, central, carry, given, sems,
):
    fetched = [pltpu.make_async_copy(initial.at[:, x], adjoint.at[:, x], sems.at[x]) for x in range(EX)]
    for x in range(3):
        fetched[x].start()
    stencil_setup(high, low)

    zero = jnp.zeros((BLOCK, BLOCK), BF16)
    h, l = split(precond[...])
    given[0:BLOCK, :] = jnp.concatenate([h, l], axis=1)
    given[BLOCK:, :] = jnp.concatenate([h, zero], axis=1)
    right = jnp.concatenate([jnp.concatenate([h, l], axis=1)] * 2, axis=0)
    stacked = jnp.concatenate([faces[...].reshape(6 * BLOCK, BLOCK), OMEGA * block_matrix[...], coupling[...]], axis=0)
    h, l = split(folded(both(stacked), right))
    for d in range(4):
        rows = slice(d * BLOCK, (d + 1) * BLOCK)
        lateral[rows, :] = jnp.concatenate([h[rows], l[rows]], axis=1)
        lateral[(d + 4) * BLOCK : (d + 5) * BLOCK, :] = jnp.concatenate([h[rows], zero], axis=1)
    parts = [slice(d * BLOCK, (d + 1) * BLOCK) for d in (6, 4, 5)]
    central[0:BLOCK, :] = jnp.concatenate([h[rows] for rows in parts] + [l[rows] for rows in parts], axis=1)
    central[BLOCK:, :] = jnp.concatenate([h[rows] for rows in parts] + [zero] * 3, axis=1)
    h, l = h[7 * BLOCK :], l[7 * BLOCK :]
    none = jnp.zeros((SPACE, 2 * BLOCK), BF16)
    carry[...] = jnp.concatenate(
        [jnp.concatenate([h, l], axis=1), none, jnp.concatenate([h, zero[:SPACE]], axis=1), none], axis=0
    )

    def enter(x):
        position = lax.broadcasted_iota(jnp.int32, (NTD, LAYER, BLOCK), 1) + x * LAYER
        fetched[x].wait()
        if x + 3 < EX:
            fetched[x + 3].start()
        value = jnp.where(position < info[0], adjoint[:, x], 0.0)
        adjoint[:, x] = value
        stencil_split(x, value, high, low)

    enter(0)
    enter(1)
    for x in layers(INNER):
        enter(x + 1)
        predict(x, field, adjoint, loads, relaxed, high, low, lateral, central, given, conductance, forcing)
    for x in range(INNER[0][0] + INNER[0][1] + 1, EX):
        enter(x)


def first_prediction(info, initial, forcing, conductance, block_matrix, precond, faces, coupling):
    return pl.pallas_call(
        first_kernel,
        out_shape=[VMEM(STACK, F32)] * 4
        + [VMEM(PADDED, BF16)] * 2
        + [VMEM(LATERAL, BF16), VMEM(CENTRAL, BF16), VMEM(SQUARE, BF16), VMEM(SQUARE, BF16)],
        in_specs=[INS, INH] + [INV] * 6,
        out_specs=[INV] * 10,
        scratch_shapes=[pltpu.SemaphoreType.DMA((EX,))],
        compiler_params=params(16),
        cost_estimate=cost(0.01),
        name="first_inner",
    )(info, initial, forcing, conductance, block_matrix, precond, faces, coupling)


def next_kernel(adjoint, loads, relaxed, lateral, central, field, high, low):
    stencil_setup(high, low)
    for x in range(2):
        stencil_split(x, adjoint[:, x], high, low)
    for x in layers(INNER):
        stencil_split(x + 1, adjoint[:, x + 1], high, low)
        predict(x, field, adjoint, loads, relaxed, high, low, lateral, central)
    for x in range(INNER[0][0] + INNER[0][1] + 1, EX):
        stencil_split(x, adjoint[:, x], high, low)


def next_prediction(adjoint, loads, relaxed, lateral, central):
    return pl.pallas_call(
        next_kernel,
        out_shape=[VMEM(STACK, F32), VMEM(PADDED, BF16), VMEM(PADDED, BF16)],
        in_specs=[INV] * 5,
        out_specs=[INV] * 3,
        compiler_params=params(16),
        cost_estimate=cost(0.01),
        name="next_inner",
    )(adjoint, loads, relaxed, lateral, central)


def rows_of(stack, t, runs):
    return jnp.concatenate([stack[t, first : first + count].reshape(count * LAYER, BLOCK) for first, count in runs], axis=0)


def chain(info, field, relaxed, carry, runs, trace, done=None):
    keep = jnp.concatenate(
        [
            (lax.broadcasted_iota(jnp.int32, (count * LAYER, BLOCK), 0) + first * LAYER < info[0]).astype(F32)
            for first, count in runs
        ],
        axis=0,
    ) > 0.5
    for t in reversed(range(NTD)):
        value = rows_of(field, t, runs)
        if trace is not None:
            value = value - rows_of(relaxed, t, runs) * folded(both(trace), carry[...])
        trace = jnp.where(keep, value, 0.0)
        at = 0
        for first, count in runs:
            rows = count * LAYER
            field[t, first : first + count] = trace[at : at + rows].reshape(count, LAYER, BLOCK)
            at += rows
        if done is not None:
            done(t)
    return trace


def packed(trace):
    half = trace.shape[0] // 2
    lane = lax.broadcasted_iota(jnp.int32, (half, BLOCK), 1)
    return jnp.where(lane < SPACE, trace[:half], pltpu.roll(trace[half:], SPACE, 1))


def unpacked(value):
    return jnp.concatenate([value, pltpu.roll(value, SPACE, 1)], axis=0)


def trace_shape(runs):
    return VMEM((len(layers(runs)) * LAYER // 2, BLOCK), F32)


def early_chain(info, field, relaxed, carry, runs, trace):
    @pl.when(info[1] == 1)
    def _():
        trace[...] = packed(chain(info, field, relaxed, carry, runs, None))

    @pl.when(info[1] == 0)
    def _():
        trace[...] = jnp.zeros(trace.shape, F32)


def face_matrix(lateral, d):
    top, bottom = pl.multiple_of(d * BLOCK, BLOCK), pl.multiple_of((d + 4) * BLOCK, BLOCK)
    return jnp.concatenate([lateral[pl.ds(top, BLOCK), :], lateral[pl.ds(bottom, BLOCK), :]], axis=0)


def inner_kernel(info, pred, relaxed, lateral, carry, y_near, y_far, field, trace):
    ((first, count),) = INNER
    for halo, at, has in ((y_near, near(info, 1), 1), (y_far, far(info, 1), info[5])):
        matrix = face_matrix(lateral, 2 + (at > 0).astype(jnp.int32))
        values = jnp.where(has > 0, halo[:, first : first + count].reshape(NTD * count * EZ, BLOCK), 0.0)
        term = folded(both(values), matrix).reshape(NTD, count, EZ, BLOCK)
        area = (slice(None), pl.ds(first, count), pl.ds(at, EZ))
        field[area] = field[area] - relaxed[area] * term
    early_chain(info, field, relaxed, carry, INNER, trace)


def inner_halos(info, field, relaxed, lateral, carry, y_halos):
    return pl.pallas_call(
        inner_kernel,
        out_shape=[VMEM(STACK, F32), trace_shape(INNER)],
        in_specs=[INS] + [INV] * 6,
        out_specs=[INV, INV],
        input_output_aliases={1: 0},
        compiler_params=params(8),
        cost_estimate=cost(2),
        name="inner_halos",
    )(info, field, relaxed, lateral, carry, *y_halos)


def outer_kernel(first_sweep, info, *refs):
    if first_sweep:
        conductance, given, forcing, *refs = refs
        (_, _, _, _, _, adjoint, lateral, central, carry, x_near, x_far, y_near, y_far,
         field, high, low, loads, relaxed, trace) = refs
    else:
        conductance = given = forcing = None
        (_, _, _, adjoint, lateral, central, carry, x_near, x_far, y_near, y_far, loads, relaxed,
         field, high, low, trace) = refs
    for halo, x, has in ((x_near, near(info, 0), 1), (x_far, far(info, 0), info[4])):
        h, l = split(jnp.where(has > 0, halo[...], 0.0))
        place = jnp.where(x > 0, EX + 1, 0)
        high[place, :, pl.ds(EZ, LAYER)] = h
        low[place, :, pl.ds(EZ, LAYER)] = l
    for halo, y, has in ((y_near, near(info, 1), 1), (y_far, far(info, 1), info[5])):
        place = pl.multiple_of(jnp.where(y > 0, LAYER + EZ, 0), EZ)
        for x in layers(OUTER):
            h, l = split(jnp.where(has > 0, halo[:, x], 0.0))
            high[x + 1, :, pl.ds(place, EZ)] = h
            low[x + 1, :, pl.ds(place, EZ)] = l
    for x in layers(OUTER):
        predict(x, field, adjoint, loads, relaxed, high, low, lateral, central, given, conductance, forcing)
    early_chain(info, field, relaxed, carry, OUTER, trace)


def outer_prediction(info, field, high, low, adjoint, lateral, central, carry, halos, loads, relaxed, given, conductance, forcing):
    first_sweep = given is not None
    if first_sweep:
        args = [info, conductance, given, forcing, field, high, low, loads, relaxed, adjoint, lateral, central, carry, *halos]
        outs = [VMEM(STACK, F32), VMEM(PADDED, BF16), VMEM(PADDED, BF16), VMEM(STACK, F32), VMEM(STACK, F32)]
        aliases = {k + 4: k for k in range(5)}
    else:
        args = [info, field, high, low, adjoint, lateral, central, carry, *halos, loads, relaxed]
        outs = [VMEM(STACK, F32), VMEM(PADDED, BF16), VMEM(PADDED, BF16)]
        aliases = {k + 1: k for k in range(3)}
    outs = outs + [trace_shape(OUTER)]
    out = pl.pallas_call(
        functools.partial(outer_kernel, first_sweep),
        out_shape=outs,
        in_specs=[INS] + [INV] * (len(args) - 1),
        out_specs=[INV] * len(outs),
        input_output_aliases=aliases,
        compiler_params=params(16),
        cost_estimate=cost(7),
        name="first_outer" if first_sweep else "next_outer",
    )(*args)
    if first_sweep:
        loads, relaxed = out[3:5]
    return out[0], out[-1], loads, relaxed


def late_chain(info, field, relaxed, carry, trace, runs):
    @pl.when(info[1] == 0)
    def _():
        chain(info, field, relaxed, carry, runs, unpacked(trace[...]))


def late_inner_kernel(info, field, relaxed, carry, trace, out):
    late_chain(info, out, relaxed, carry, trace, INNER)


def late_outer_kernel(info, field, relaxed, carry, trace, out, x_near, x_far, y_near, y_far):
    late_chain(info, out, relaxed, carry, trace, OUTER)
    x_near[...] = out[:, near(info, 0)]
    x_far[...] = out[:, far(info, 0)]
    y_near[...] = out[:, :, pl.ds(near(info, 1), EZ)]
    y_far[...] = out[:, :, pl.ds(far(info, 1), EZ)]


def after_trace(info, field, relaxed, carry, trace, inner):
    outs = [VMEM(STACK, F32)] + ([] if inner else FACES)
    return pl.pallas_call(
        late_inner_kernel if inner else late_outer_kernel,
        out_shape=outs,
        in_specs=[INS] + [INV] * 4,
        out_specs=[INV] * len(outs),
        input_output_aliases={1: 0},
        compiler_params=params(8),
        cost_estimate=cost(2),
        name="late_inner" if inner else "late_outer",
    )(info, field, relaxed, carry, trace)


def last_chain(info, relaxed, carry, trace, kept, out, sems, runs):
    copies = [
        [
            pltpu.make_async_copy(kept.at[t, pl.ds(first, count)], out.at[t, pl.ds(first, count)], sems.at[t, k])
            for k, (first, count) in enumerate(runs)
        ]
        for t in range(NTD)
    ]

    def send(t):
        for copy in copies[t]:
            copy.start()

    @pl.when(info[1] == 0)
    def _():
        chain(info, kept, relaxed, carry, runs, unpacked(trace[...]), send)

    @pl.when(info[1] == 1)
    def _():
        for t in range(NTD):
            send(t)

    for t in range(NTD):
        for copy in copies[t]:
            copy.wait()


def last_inner_kernel(info, field, relaxed, carry, trace, kept, out, sems):
    last_chain(info, relaxed, carry, trace, kept, out, sems, INNER)


def last_outer_kernel(info, field, relaxed, carry, trace, given, kept, out, sems):
    last_chain(info, relaxed, carry, trace, kept, out, sems, OUTER)


def last(info, field, relaxed, carry, trace, given):
    inner = given is None
    args = [info, field, relaxed, carry, trace] + ([] if inner else [given])
    return pl.pallas_call(
        last_inner_kernel if inner else last_outer_kernel,
        out_shape=[VMEM(STACK, F32), pltpu.HBM(STACK, F32)],
        in_specs=[INS] + [INV] * 4 + ([] if inner else [INH]),
        out_specs=[INV, INH],
        input_output_aliases={1: 0} if inner else {1: 0, 5: 1},
        scratch_shapes=[pltpu.SemaphoreType.DMA((NTD, 2))],
        compiler_params=params(8),
        cost_estimate=cost(3),
        name="last_inner" if inner else "last_outer",
    )(*args)


def both_ways(pairs):
    return pairs + [(j, i) for i, j in pairs]


def exchanged(value, axis, first):
    count = lax.axis_size(axis)
    return lax.ppermute(value, axis, both_ways([(i, (i + 1) % count) for i in range(first, count, 2)]))


def exchanged_far_x(value):
    count, lines = lax.axis_size("sx"), lax.axis_size("sy")
    pairs = [(i * lines + k, (i + 1) * lines + k) for i in range(1, count - 1, 2) for k in range(lines)]
    pairs += [(i * lines + k, i * lines + k + 1) for i in (0, count - 1) for k in range(0, lines, 2)]
    return lax.ppermute(value, ("sx", "sy"), both_ways(pairs))


def sent_back(value):
    return lax.ppermute(value, "tm", [(1, 0), (0, 1)])


def body(forcing, initial, conductance, counts, block_matrix, precond, face_coupling, time_coupling):
    shape = forcing.shape
    in_hbm = functools.partial(pltpu.with_memory_space_constraint, memory_space=pltpu.HBM)
    forcing, initial = forcing.reshape(STACK), in_hbm(initial.reshape(STACK))
    even_x = 1 - lax.rem(lax.axis_index("sx"), 2).astype(jnp.int32)
    even_y = 1 - lax.rem(lax.axis_index("sy"), 2).astype(jnp.int32)
    at_x, at_y = lax.axis_index("sx"), lax.axis_index("sy")
    has_x = jnp.logical_and(at_x > 0, at_x < lax.axis_size("sx") - 1).astype(jnp.int32)
    has_y = jnp.logical_and(at_y > 0, at_y < lax.axis_size("sy") - 1).astype(jnp.int32)
    info = jnp.stack(
        [
            counts[0, 0], lax.axis_index("tm").astype(jnp.int32),
            even_x * (EX - 1), even_y * (LAYER - EZ), has_x, has_y,
        ]
    )

    def halos_of(x_near, x_far, y_near, y_far):
        return (
            exchanged(x_near, "sx", 0), exchanged_far_x(x_far),
            exchanged(y_near, "sy", 0), exchanged(y_far, "sy", 1),
        )

    halos = halos_of(*faces_of_initial(info, initial))
    field, adjoint, loads, relaxed, high, low, lateral, central, carry, given = first_prediction(
        info, initial, forcing, conductance, block_matrix, precond, face_coupling, time_coupling
    )
    for sweep in range(SWEEPS):
        if sweep:
            adjoint, given = field, None
            field, high, low = next_prediction(adjoint, loads, relaxed, lateral, central)
        field, inner = inner_halos(info, field, relaxed, lateral, carry, halos[2:])
        inner = sent_back(inner)
        field, outer, loads, relaxed = outer_prediction(
            info, field, high, low, adjoint, lateral, central, carry, halos, loads, relaxed, given, conductance, forcing
        )
        outer = sent_back(outer)
        if sweep < SWEEPS - 1:
            (field,) = after_trace(info, field, relaxed, carry, inner, True)
            field, *faces = after_trace(info, field, relaxed, carry, outer, False)
            halos = halos_of(*faces)
        else:
            field, out = last(info, field, relaxed, carry, inner, None)
            field, out = last(info, field, relaxed, carry, outer, out)
    return out.reshape(shape)


def solution(mesh):
    in_specs = (
        P("tm", "sx", "sy", None, None),
        P("tm", "sx", "sy", None, None),
        P("tm", "sx", "sy", None),
        P("sx", "sy"),
        P(),
        P(),
        P(),
        P(),
    )
    out_specs = P("tm", "sx", "sy", None, None)
    return jax.shard_map(body, mesh=mesh, in_specs=in_specs, out_specs=out_specs, check_vma=False)
```

```python
import functools

import jax
import jax.numpy as jnp
from jax import lax
from jax.experimental import pallas as pl
from jax.experimental.pallas import tpu as pltpu
from jax.sharding import PartitionSpec as P

SWEEPS = 2
OMEGA = 0.7
NTD, EX, EY, EZ, BLOCK = 4, 8, 16, 16, 128
SPACE = BLOCK // 2
LAYER = EY * EZ
F32, BF16 = jnp.float32, jnp.bfloat16
VMEM = pltpu.VMEM
ANY = pl.BlockSpec(memory_space=pl.ANY)
INH = pl.BlockSpec(memory_space=pltpu.HBM)
INV = pl.BlockSpec(memory_space=VMEM)
INNER = ((1, 5),)
OUTER = ((0, 1), (6, 2))
NEXT_INNER = ((1, 6),)
NEXT_OUTER = ((0, 1), (7, 1))


def params(mib):
    return pltpu.CompilerParams(vmem_limit_bytes=mib << 20)


def cost(us):
    return pl.CostEstimate(flops=int(us * 1.0e9), bytes_accessed=0, transcendentals=0)


def split(value):
    high = value.astype(BF16)
    low = (value - high.astype(F32)).astype(BF16)
    return high, low


def dot(rows, matrix):
    return jnp.dot(rows, matrix, preferred_element_type=F32)


def both(value):
    return jnp.concatenate(split(value), axis=-1)


def folded(rows, matrix):
    out = dot(rows, matrix)
    return out[:, :BLOCK] + out[:, BLOCK:]


def mask(info, first, rows):
    position = lax.broadcasted_iota(jnp.int32, (rows, BLOCK), 0) + first * LAYER
    return position < info[0]


def facts(count):
    at_x, at_y = lax.axis_index("sx"), lax.axis_index("sy")
    return (
        count[0:1, :],
        lax.axis_index("tm"),
        jnp.where(lax.rem(at_x, 2) == 0, EX - 1, 0),
        jnp.where(lax.rem(at_y, 2) == 0, LAYER - EZ, 0),
        jnp.logical_and(at_x > 0, at_x < lax.axis_size("sx") - 1).astype(jnp.int32),
        jnp.logical_and(at_y > 0, at_y < lax.axis_size("sy") - 1).astype(jnp.int32),
    )


def near(info, dim):
    return pl.multiple_of(info[3], EZ) if dim else info[2]


def far(info, dim):
    return pl.multiple_of(LAYER - EZ - info[3], EZ) if dim else EX - 1 - info[2]


def faces_kernel(info, initial, x_near, x_far, y_near, y_far, sems):
    info = facts(info)
    places = (near(info, 0), far(info, 0), near(info, 1), far(info, 1))
    refs = (x_near, x_far, y_near, y_far)
    copies = [
        pltpu.make_async_copy(initial.at[:, at] if k < 2 else initial.at[:, :, pl.ds(at, EZ)], ref, sems.at[k])
        for k, (ref, at) in enumerate(zip(refs, places))
    ]
    for copy in copies:
        copy.start()
    for copy, ref, at in zip(copies[:2], refs[:2], places[:2]):
        copy.wait()
        keep = mask(info, at, LAYER)
        for t in range(NTD):
            ref[t] = jnp.where(keep, ref[t], 0.0)
    for copy, ref, at in zip(copies[2:], refs[2:], places[2:]):
        copy.wait()
        for x in range(EX):
            position = lax.broadcasted_iota(jnp.int32, (EZ, BLOCK), 0) + (x * LAYER + at)
            for t in range(NTD):
                ref[t, x] = jnp.where(position < info[0], ref[t, x], 0.0)


FACES = [VMEM((NTD, LAYER, BLOCK), F32)] * 2 + [VMEM((NTD, EX, EZ, BLOCK), F32)] * 2


def faces_of_initial(info, initial):
    return pl.pallas_call(
        faces_kernel,
        out_shape=FACES,
        in_specs=[INV, INH],
        out_specs=[INV] * 4,
        scratch_shapes=[pltpu.SemaphoreType.DMA((4,))],
        compiler_params=params(4),
        cost_estimate=cost(2),
        name="faces",
    )(info, initial)


def stencil_setup(high, low):
    for ref in (high, low):
        for x in (0, EX + 1):
            ref[x] = jnp.zeros(ref.shape[1:], BF16)
        for x in range(1, EX + 1):
            for t in range(NTD):
                ref[x, t, 0:EZ] = jnp.zeros((EZ, BLOCK), BF16)
                ref[x, t, EZ + LAYER :] = jnp.zeros((EZ, BLOCK), BF16)


def stencil_split(x, value, high, low):
    h, l = split(value)
    high[x + 1, :, pl.ds(EZ, LAYER)] = h
    low[x + 1, :, pl.ds(EZ, LAYER)] = l


def flat(value):
    return value.reshape(NTD * LAYER, BLOCK)


def stencil_layer(x, adjoint, high, low, lateral, central):
    pieces = []
    for ref in (high, low):
        pieces += [
            flat(ref[x, :, pl.ds(EZ, LAYER)]),
            flat(ref[x + 2, :, pl.ds(EZ, LAYER)]),
            flat(ref[x + 1, :, pl.ds(0, LAYER)]),
            flat(ref[x + 1, :, pl.ds(2 * EZ, LAYER)]),
        ]
    around = folded(jnp.concatenate(pieces, axis=1), lateral[...])
    own = [flat(ref[x + 1, :, pl.ds(EZ, LAYER)]) for ref in (high, low)]
    out = dot(jnp.concatenate(own, axis=1), central[...])
    own, below, above = (
        out[:, k * BLOCK : (k + 1) * BLOCK] + out[:, (k + 3) * BLOCK : (k + 4) * BLOCK] for k in range(3)
    )
    depth = lax.broadcasted_iota(jnp.int32, (NTD * LAYER, BLOCK), 0) % EZ
    below = jnp.where(depth == 0, 0.0, pltpu.roll(below, 1, 0))
    above = jnp.where(depth == EZ - 1, 0.0, pltpu.roll(above, NTD * LAYER - 1, 0))
    return adjoint - own, around + below + above


STACK = (NTD, EX, LAYER, BLOCK)
PADDED = (EX + 2, NTD, LAYER + 2 * EZ, BLOCK)
LATERAL = (8 * BLOCK, 2 * BLOCK)
CENTRAL = (2 * BLOCK, 6 * BLOCK)
SQUARE = (2 * BLOCK, 2 * BLOCK)


def layers(runs):
    return [x for first, count in runs for x in range(first, first + count)]


def row_factors(conductance, x, relaxed):
    factor = []
    for t in range(NTD):
        inverse = OMEGA / conductance[t, x]
        spread = jnp.broadcast_to(inverse[:, None, :], (EY, EZ, EZ)).reshape(LAYER, EZ)
        lane = lax.broadcasted_iota(jnp.int32, (LAYER, EZ), 1)
        depth = lax.broadcasted_iota(jnp.int32, (LAYER, EZ), 0) % EZ
        column = jnp.sum(jnp.where(lane == depth, spread, 0.0), axis=1, keepdims=True)
        column = jnp.broadcast_to(column, (LAYER, BLOCK))
        relaxed[t, x] = column
        factor.append(column)
    return jnp.concatenate(factor, axis=0)


def predict(x, field, adjoint, loads, relaxed, high, low, lateral, central, given=None, conductance=None, forcing=None):
    if given is None:
        factor, rest = flat(relaxed[:, x]), flat(loads[:, x])
    else:
        factor = row_factors(conductance, x, relaxed)
        rest = factor * folded(both(flat(forcing[:, x])), given[...])
        loads[:, x] = rest.reshape(NTD, LAYER, BLOCK)
    own, around = stencil_layer(x, flat(adjoint[:, x]), high, low, lateral, central)
    field[:, x] = (own + rest - factor * around).reshape(NTD, LAYER, BLOCK)


def first_kernel(
    info, initial, forcing, conductance, block_matrix, precond, faces, coupling,
    field, adjoint, loads, relaxed, high, low, lateral, central, carry, given, sems,
):
    info = facts(info)
    fetched = [pltpu.make_async_copy(initial.at[:, x], adjoint.at[:, x], sems.at[x]) for x in range(EX)]
    for x in range(3):
        fetched[x].start()
    stencil_setup(high, low)

    zero = jnp.zeros((BLOCK, BLOCK), BF16)
    h, l = split(precond[...])
    given[0:BLOCK, :] = jnp.concatenate([h, l], axis=1)
    given[BLOCK:, :] = jnp.concatenate([h, zero], axis=1)
    right = jnp.concatenate([jnp.concatenate([h, l], axis=1)] * 2, axis=0)
    stacked = jnp.concatenate([faces[...].reshape(6 * BLOCK, BLOCK), OMEGA * block_matrix[...], coupling[...]], axis=0)
    h, l = split(folded(both(stacked), right))
    for d in range(4):
        rows = slice(d * BLOCK, (d + 1) * BLOCK)
        lateral[rows, :] = jnp.concatenate([h[rows], l[rows]], axis=1)
        lateral[(d + 4) * BLOCK : (d + 5) * BLOCK, :] = jnp.concatenate([h[rows], zero], axis=1)
    parts = [slice(d * BLOCK, (d + 1) * BLOCK) for d in (6, 4, 5)]
    central[0:BLOCK, :] = jnp.concatenate([h[rows] for rows in parts] + [l[rows] for rows in parts], axis=1)
    central[BLOCK:, :] = jnp.concatenate([h[rows] for rows in parts] + [zero] * 3, axis=1)
    h, l = h[7 * BLOCK :], l[7 * BLOCK :]
    none = jnp.zeros((SPACE, 2 * BLOCK), BF16)
    carry[...] = jnp.concatenate(
        [jnp.concatenate([h, l], axis=1), none, jnp.concatenate([h, zero[:SPACE]], axis=1), none], axis=0
    )

    def enter(x):
        position = lax.broadcasted_iota(jnp.int32, (NTD, LAYER, BLOCK), 1) + x * LAYER
        fetched[x].wait()
        if x + 3 < EX:
            fetched[x + 3].start()
        value = jnp.where(position < info[0], adjoint[:, x], 0.0)
        adjoint[:, x] = value
        stencil_split(x, value, high, low)

    enter(0)
    enter(1)
    for x in layers(INNER):
        enter(x + 1)
        predict(x, field, adjoint, loads, relaxed, high, low, lateral, central, given, conductance, forcing)
    for x in range(INNER[0][0] + INNER[0][1] + 1, EX):
        enter(x)


def first_prediction(info, initial, forcing, conductance, block_matrix, precond, faces, coupling):
    return pl.pallas_call(
        first_kernel,
        out_shape=[VMEM(STACK, F32)] * 4
        + [VMEM(PADDED, BF16)] * 2
        + [VMEM(LATERAL, BF16), VMEM(CENTRAL, BF16), VMEM(SQUARE, BF16), VMEM(SQUARE, BF16)],
        in_specs=[INV, INH] + [INV] * 6,
        out_specs=[INV] * 10,
        scratch_shapes=[pltpu.SemaphoreType.DMA((EX,))],
        compiler_params=params(16),
        cost_estimate=cost(0.01),
        name="first_inner",
    )(info, initial, forcing, conductance, block_matrix, precond, faces, coupling)


def next_kernel(adjoint, loads, relaxed, lateral, central, field, high, low):
    stencil_setup(high, low)
    for x in range(2):
        stencil_split(x, adjoint[:, x], high, low)
    for x in layers(NEXT_INNER):
        stencil_split(x + 1, adjoint[:, x + 1], high, low)
        predict(x, field, adjoint, loads, relaxed, high, low, lateral, central)


def next_prediction(adjoint, loads, relaxed, lateral, central):
    return pl.pallas_call(
        next_kernel,
        out_shape=[VMEM(STACK, F32), VMEM(PADDED, BF16), VMEM(PADDED, BF16)],
        in_specs=[INV] * 5,
        out_specs=[INV] * 3,
        compiler_params=params(16),
        cost_estimate=cost(0.01),
        name="next_inner",
    )(adjoint, loads, relaxed, lateral, central)


def rows_of(stack, t, runs):
    return jnp.concatenate([stack[t, first : first + count].reshape(count * LAYER, BLOCK) for first, count in runs], axis=0)


def chain(info, field, relaxed, carry, runs, trace, done=None):
    keep = jnp.concatenate(
        [
            (lax.broadcasted_iota(jnp.int32, (count * LAYER, BLOCK), 0) + first * LAYER < info[0]).astype(F32)
            for first, count in runs
        ],
        axis=0,
    ) > 0.5
    for t in reversed(range(NTD)):
        value = rows_of(field, t, runs)
        if trace is not None:
            value = value - rows_of(relaxed, t, runs) * folded(both(trace), carry[...])
        trace = jnp.where(keep, value, 0.0)
        at = 0
        for first, count in runs:
            rows = count * LAYER
            field[t, first : first + count] = trace[at : at + rows].reshape(count, LAYER, BLOCK)
            at += rows
        if done is not None:
            done(t)
    return trace


def packed(trace):
    half = trace.shape[0] // 2
    lane = lax.broadcasted_iota(jnp.int32, (half, BLOCK), 1)
    return jnp.where(lane < SPACE, trace[:half], pltpu.roll(trace[half:], SPACE, 1))


def unpacked(value):
    return jnp.concatenate([value, pltpu.roll(value, SPACE, 1)], axis=0)


def trace_shape(runs):
    return VMEM((len(layers(runs)) * LAYER // 2, BLOCK), F32)


def early_chain(info, field, relaxed, carry, runs, trace):
    @pl.when(info[1] == 1)
    def _():
        trace[...] = packed(chain(info, field, relaxed, carry, runs, None))

    @pl.when(info[1] == 0)
    def _():
        trace[...] = jnp.zeros(trace.shape, F32)


def face_matrix(lateral, d):
    top, bottom = pl.multiple_of(d * BLOCK, BLOCK), pl.multiple_of((d + 4) * BLOCK, BLOCK)
    return jnp.concatenate([lateral[pl.ds(top, BLOCK), :], lateral[pl.ds(bottom, BLOCK), :]], axis=0)


def inner_kernel(predicted, info, pred, relaxed, lateral, carry, y_near, y_far, field, trace):
    info = facts(info)
    ((first, count),) = predicted
    for halo, at, has in ((y_near, near(info, 1), 1), (y_far, far(info, 1), info[5])):
        matrix = face_matrix(lateral, 2 + (at > 0).astype(jnp.int32))
        values = jnp.where(has > 0, halo[:, first : first + count].reshape(NTD * count * EZ, BLOCK), 0.0)
        term = folded(both(values), matrix).reshape(NTD, count, EZ, BLOCK)
        area = (slice(None), pl.ds(first, count), pl.ds(at, EZ))
        field[area] = field[area] - relaxed[area] * term
    early_chain(info, field, relaxed, carry, INNER, trace)


def inner_halos(info, field, relaxed, lateral, carry, y_halos, predicted):
    return pl.pallas_call(
        functools.partial(inner_kernel, predicted),
        out_shape=[VMEM(STACK, F32), trace_shape(INNER)],
        in_specs=[INV] + [INV] * 6,
        out_specs=[INV, INV],
        input_output_aliases={1: 0},
        compiler_params=params(8),
        cost_estimate=cost(2),
        name="inner_halos",
    )(info, field, relaxed, lateral, carry, *y_halos)


def outer_kernel(first_sweep, info, *refs):
    info = facts(info)
    predicted = OUTER if first_sweep else NEXT_OUTER
    if first_sweep:
        conductance, given, forcing, *refs = refs
        (_, _, _, _, _, adjoint, lateral, central, carry, x_near, x_far, y_near, y_far,
         field, high, low, loads, relaxed, trace) = refs
    else:
        conductance = given = forcing = None
        (_, _, _, adjoint, lateral, central, carry, x_near, x_far, y_near, y_far, loads, relaxed,
         field, high, low, trace) = refs
    for halo, x, has in ((x_near, near(info, 0), 1), (x_far, far(info, 0), info[4])):
        h, l = split(jnp.where(has > 0, halo[...], 0.0))
        place = jnp.where(x > 0, EX + 1, 0)
        high[place, :, pl.ds(EZ, LAYER)] = h
        low[place, :, pl.ds(EZ, LAYER)] = l
    for halo, y, has in ((y_near, near(info, 1), 1), (y_far, far(info, 1), info[5])):
        place = pl.multiple_of(jnp.where(y > 0, LAYER + EZ, 0), EZ)
        for x in layers(predicted):
            h, l = split(jnp.where(has > 0, halo[:, x], 0.0))
            high[x + 1, :, pl.ds(place, EZ)] = h
            low[x + 1, :, pl.ds(place, EZ)] = l
    for x in layers(predicted):
        predict(x, field, adjoint, loads, relaxed, high, low, lateral, central, given, conductance, forcing)
    early_chain(info, field, relaxed, carry, OUTER, trace)


def outer_prediction(info, field, high, low, adjoint, lateral, central, carry, halos, loads, relaxed, given, conductance, forcing):
    first_sweep = given is not None
    if first_sweep:
        args = [info, conductance, given, forcing, field, high, low, loads, relaxed, adjoint, lateral, central, carry, *halos]
        outs = [VMEM(STACK, F32), VMEM(PADDED, BF16), VMEM(PADDED, BF16), VMEM(STACK, F32), VMEM(STACK, F32)]
        aliases = {k + 4: k for k in range(5)}
    else:
        args = [info, field, high, low, adjoint, lateral, central, carry, *halos, loads, relaxed]
        outs = [VMEM(STACK, F32), VMEM(PADDED, BF16), VMEM(PADDED, BF16)]
        aliases = {k + 1: k for k in range(3)}
    outs = outs + [trace_shape(OUTER)]
    out = pl.pallas_call(
        functools.partial(outer_kernel, first_sweep),
        out_shape=outs,
        in_specs=[INV] + [INV] * (len(args) - 1),
        out_specs=[INV] * len(outs),
        input_output_aliases=aliases,
        compiler_params=params(16),
        cost_estimate=cost(7),
        name="first_outer" if first_sweep else "next_outer",
    )(*args)
    if first_sweep:
        loads, relaxed = out[3:5]
    return out[0], out[-1], loads, relaxed


def late_chain(info, field, relaxed, carry, trace, runs):
    @pl.when(info[1] == 0)
    def _():
        chain(info, field, relaxed, carry, runs, unpacked(trace[...]))


def late_inner_kernel(info, field, relaxed, carry, trace, out):
    info = facts(info)
    late_chain(info, out, relaxed, carry, trace, INNER)


def late_outer_kernel(info, field, relaxed, carry, trace, out, x_near, x_far, y_near, y_far):
    info = facts(info)
    late_chain(info, out, relaxed, carry, trace, OUTER)
    x_near[...] = out[:, near(info, 0)]
    x_far[...] = out[:, far(info, 0)]
    y_near[...] = out[:, :, pl.ds(near(info, 1), EZ)]
    y_far[...] = out[:, :, pl.ds(far(info, 1), EZ)]


def after_trace(info, field, relaxed, carry, trace, inner):
    outs = [VMEM(STACK, F32)] + ([] if inner else FACES)
    return pl.pallas_call(
        late_inner_kernel if inner else late_outer_kernel,
        out_shape=outs,
        in_specs=[INV] + [INV] * 4,
        out_specs=[INV] * len(outs),
        input_output_aliases={1: 0},
        compiler_params=params(8),
        cost_estimate=cost(2),
        name="late_inner" if inner else "late_outer",
    )(info, field, relaxed, carry, trace)


def last_chain(info, relaxed, carry, trace, kept, out, sems, runs):
    copies = [
        [
            pltpu.make_async_copy(kept.at[t, pl.ds(first, count)], out.at[t, pl.ds(first, count)], sems.at[t, k])
            for k, (first, count) in enumerate(runs)
        ]
        for t in range(NTD)
    ]

    def send(t):
        for copy in copies[t]:
            copy.start()

    @pl.when(info[1] == 0)
    def _():
        chain(info, kept, relaxed, carry, runs, unpacked(trace[...]), send)

    @pl.when(info[1] == 1)
    def _():
        for t in range(NTD):
            send(t)

    for t in range(NTD):
        for copy in copies[t]:
            copy.wait()


def last_inner_kernel(info, field, relaxed, carry, trace, kept, out, sems):
    info = facts(info)
    last_chain(info, relaxed, carry, trace, kept, out, sems, INNER)


def last_outer_kernel(info, field, relaxed, carry, trace, given, kept, out, sems):
    info = facts(info)
    last_chain(info, relaxed, carry, trace, kept, out, sems, OUTER)


def last(info, field, relaxed, carry, trace, given):
    inner = given is None
    args = [info, field, relaxed, carry, trace] + ([] if inner else [given])
    return pl.pallas_call(
        last_inner_kernel if inner else last_outer_kernel,
        out_shape=[VMEM(STACK, F32), pltpu.HBM(STACK, F32)],
        in_specs=[INV] + [INV] * 4 + ([] if inner else [INH]),
        out_specs=[INV, INH],
        input_output_aliases={1: 0} if inner else {1: 0, 5: 1},
        scratch_shapes=[pltpu.SemaphoreType.DMA((NTD, 2))],
        compiler_params=params(8),
        cost_estimate=cost(3),
        name="last_inner" if inner else "last_outer",
    )(*args)


def both_ways(pairs):
    return pairs + [(j, i) for i, j in pairs]


def exchanged(value, axis, first):
    count = lax.axis_size(axis)
    return lax.ppermute(value, axis, both_ways([(i, (i + 1) % count) for i in range(first, count, 2)]))


def exchanged_far_x(value):
    count, lines = lax.axis_size("sx"), lax.axis_size("sy")
    pairs = [(i * lines + k, (i + 1) * lines + k) for i in range(1, count - 1, 2) for k in range(lines)]
    pairs += [(i * lines + k, i * lines + k + 1) for i in (0, count - 1) for k in range(0, lines, 2)]
    return lax.ppermute(value, ("sx", "sy"), both_ways(pairs))


def sent_back(value):
    return lax.ppermute(value, "tm", [(1, 0), (0, 1)])


def body(forcing, initial, conductance, counts, block_matrix, precond, face_coupling, time_coupling):
    shape = forcing.shape
    in_hbm = functools.partial(pltpu.with_memory_space_constraint, memory_space=pltpu.HBM)
    forcing, initial = forcing.reshape(STACK), in_hbm(initial.reshape(STACK))
    info = jnp.full((8, BLOCK), counts[0, 0])

    def halos_of(x_near, x_far, y_near, y_far):
        return (
            exchanged(x_near, "sx", 0), exchanged_far_x(x_far),
            exchanged(y_near, "sy", 0), exchanged(y_far, "sy", 1),
        )

    halos = halos_of(*faces_of_initial(info, initial))
    field, adjoint, loads, relaxed, high, low, lateral, central, carry, given = first_prediction(
        info, initial, forcing, conductance, block_matrix, precond, face_coupling, time_coupling
    )
    for sweep in range(SWEEPS):
        if sweep:
            adjoint, given = field, None
            field, high, low = next_prediction(adjoint, loads, relaxed, lateral, central)
        field, inner = inner_halos(
            info, field, relaxed, lateral, carry, halos[2:], NEXT_INNER if sweep else INNER
        )
        inner = sent_back(inner)
        field, outer, loads, relaxed = outer_prediction(
            info, field, high, low, adjoint, lateral, central, carry, halos, loads, relaxed, given, conductance, forcing
        )
        outer = sent_back(outer)
        if sweep < SWEEPS - 1:
            (field,) = after_trace(info, field, relaxed, carry, inner, True)
            field, *faces = after_trace(info, field, relaxed, carry, outer, False)
            halos = halos_of(*faces)
        else:
            field, out = last(info, field, relaxed, carry, inner, None)
            field, out = last(info, field, relaxed, carry, outer, out)
    return out.reshape(shape)


def solution(mesh):
    in_specs = (
        P("tm", "sx", "sy", None, None),
        P("tm", "sx", "sy", None, None),
        P("tm", "sx", "sy", None),
        P("sx", "sy"),
        P(),
        P(),
        P(),
        P(),
    )
    out_specs = P("tm", "sx", "sy", None, None)
    return jax.shard_map(body, mesh=mesh, in_specs=in_specs, out_specs=out_specs, check_vma=False)
```

```python
import functools

import jax
import jax.numpy as jnp
from jax import lax
from jax.experimental import pallas as pl
from jax.experimental.pallas import tpu as pltpu
from jax.sharding import PartitionSpec as P

SWEEPS = 2
OMEGA = 0.7
NTD, EX, EY, EZ, BLOCK = 4, 8, 16, 16, 128
SPACE = BLOCK // 2
LAYER = EY * EZ
F32, BF16 = jnp.float32, jnp.bfloat16
VMEM = pltpu.VMEM
ANY = pl.BlockSpec(memory_space=pl.ANY)
INH = pl.BlockSpec(memory_space=pltpu.HBM)
INV = pl.BlockSpec(memory_space=VMEM)
INNER = ((1, 5),)
OUTER = ((0, 1), (6, 2))
NEXT_INNER = ((1, 6),)
NEXT_OUTER = ((0, 1), (7, 1))


def params(mib):
    return pltpu.CompilerParams(vmem_limit_bytes=mib << 20)


def cost(us):
    return pl.CostEstimate(flops=int(us * 1.0e9), bytes_accessed=0, transcendentals=0)


def split(value):
    high = value.astype(BF16)
    low = (value - high.astype(F32)).astype(BF16)
    return high, low


def dot(rows, matrix):
    return jnp.dot(rows, matrix, preferred_element_type=F32)


def both(value):
    return jnp.concatenate(split(value), axis=-1)


def folded(rows, matrix):
    out = dot(rows, matrix)
    return out[:, :BLOCK] + out[:, BLOCK:]


def mask(info, first, rows):
    position = lax.broadcasted_iota(jnp.int32, (rows, BLOCK), 0) + first * LAYER
    return position < info[0]


def facts(count):
    at_x, at_y = lax.axis_index("sx"), lax.axis_index("sy")
    return (
        count[0:1, :],
        lax.axis_index("tm"),
        jnp.where(lax.rem(at_x, 2) == 0, EX - 1, 0),
        jnp.where(lax.rem(at_y, 2) == 0, LAYER - EZ, 0),
        jnp.logical_and(at_x > 0, at_x < lax.axis_size("sx") - 1).astype(jnp.int32),
        jnp.logical_and(at_y > 0, at_y < lax.axis_size("sy") - 1).astype(jnp.int32),
    )


def near(info, dim):
    return pl.multiple_of(info[3], EZ) if dim else info[2]


def far(info, dim):
    return pl.multiple_of(LAYER - EZ - info[3], EZ) if dim else EX - 1 - info[2]


def faces_kernel(info, initial, x_near, x_far, y_near, y_far, sems):
    info = facts(info)
    places = (near(info, 0), far(info, 0), near(info, 1), far(info, 1))
    refs = (x_near, x_far, y_near, y_far)
    copies = [
        pltpu.make_async_copy(initial.at[:, at] if k < 2 else initial.at[:, :, pl.ds(at, EZ)], ref, sems.at[k])
        for k, (ref, at) in enumerate(zip(refs, places))
    ]
    for copy in copies:
        copy.start()
    for copy, ref, at in zip(copies[:2], refs[:2], places[:2]):
        copy.wait()
        keep = mask(info, at, LAYER)
        for t in range(NTD):
            ref[t] = jnp.where(keep, ref[t], 0.0)
    for copy, ref, at in zip(copies[2:], refs[2:], places[2:]):
        copy.wait()
        for x in range(EX):
            position = lax.broadcasted_iota(jnp.int32, (EZ, BLOCK), 0) + (x * LAYER + at)
            for t in range(NTD):
                ref[t, x] = jnp.where(position < info[0], ref[t, x], 0.0)


FACES = [VMEM((NTD, LAYER, BLOCK), F32)] * 2 + [VMEM((NTD, EX, EZ, BLOCK), F32)] * 2


def faces_of_initial(info, initial):
    return pl.pallas_call(
        faces_kernel,
        out_shape=FACES,
        in_specs=[INV, INH],
        out_specs=[INV] * 4,
        scratch_shapes=[pltpu.SemaphoreType.DMA((4,))],
        compiler_params=params(4),
        cost_estimate=cost(2),
        name="faces",
    )(info, initial)


def stencil_setup(high, low):
    for ref in (high, low):
        for x in (0, EX + 1):
            ref[x] = jnp.zeros(ref.shape[1:], BF16)
        for x in range(1, EX + 1):
            for t in range(NTD):
                ref[x, t, 0:EZ] = jnp.zeros((EZ, BLOCK), BF16)
                ref[x, t, EZ + LAYER :] = jnp.zeros((EZ, BLOCK), BF16)


def stencil_split(x, value, high, low):
    h, l = split(value)
    high[x + 1, :, pl.ds(EZ, LAYER)] = h
    low[x + 1, :, pl.ds(EZ, LAYER)] = l


def flat(value):
    return value.reshape(NTD * LAYER, BLOCK)


def stencil_layer(x, adjoint, high, low, lateral, central):
    pieces = []
    for ref in (high, low):
        pieces += [
            flat(ref[x, :, pl.ds(EZ, LAYER)]),
            flat(ref[x + 2, :, pl.ds(EZ, LAYER)]),
            flat(ref[x + 1, :, pl.ds(0, LAYER)]),
            flat(ref[x + 1, :, pl.ds(2 * EZ, LAYER)]),
        ]
    around = folded(jnp.concatenate(pieces, axis=1), lateral[...])
    own = [flat(ref[x + 1, :, pl.ds(EZ, LAYER)]) for ref in (high, low)]
    out = dot(jnp.concatenate(own, axis=1), central[...])
    own, below, above = (
        out[:, k * BLOCK : (k + 1) * BLOCK] + out[:, (k + 3) * BLOCK : (k + 4) * BLOCK] for k in range(3)
    )
    depth = lax.broadcasted_iota(jnp.int32, (NTD * LAYER, BLOCK), 0) % EZ
    below = jnp.where(depth == 0, 0.0, pltpu.roll(below, 1, 0))
    above = jnp.where(depth == EZ - 1, 0.0, pltpu.roll(above, NTD * LAYER - 1, 0))
    return adjoint - own, around + below + above


STACK = (NTD, EX, LAYER, BLOCK)
PADDED = (EX + 2, NTD, LAYER + 2 * EZ, BLOCK)
LATERAL = (8 * BLOCK, 2 * BLOCK)
CENTRAL = (2 * BLOCK, 6 * BLOCK)
SQUARE = (2 * BLOCK, 2 * BLOCK)


def layers(runs):
    return [x for first, count in runs for x in range(first, first + count)]


def row_factors(conductance, x, relaxed):
    factor = []
    for t in range(NTD):
        inverse = OMEGA / conductance[t, x]
        spread = jnp.broadcast_to(inverse[:, None, :], (EY, EZ, EZ)).reshape(LAYER, EZ)
        lane = lax.broadcasted_iota(jnp.int32, (LAYER, EZ), 1)
        depth = lax.broadcasted_iota(jnp.int32, (LAYER, EZ), 0) % EZ
        column = jnp.sum(jnp.where(lane == depth, spread, 0.0), axis=1, keepdims=True)
        column = jnp.broadcast_to(column, (LAYER, BLOCK))
        relaxed[t, x] = column
        factor.append(column)
    return jnp.concatenate(factor, axis=0)


def predict(x, field, adjoint, loads, relaxed, high, low, lateral, central, given=None, conductance=None, forcing=None):
    if given is None:
        factor, rest = flat(relaxed[:, x]), flat(loads[:, x])
    else:
        factor = row_factors(conductance, x, relaxed)
        rest = factor * folded(both(flat(forcing[:, x])), given[...])
        loads[:, x] = rest.reshape(NTD, LAYER, BLOCK)
    own, around = stencil_layer(x, flat(adjoint[:, x]), high, low, lateral, central)
    field[:, x] = (own + rest - factor * around).reshape(NTD, LAYER, BLOCK)


def first_kernel(
    info, initial, forcing, conductance, block_matrix, precond, faces, coupling,
    field, adjoint, loads, relaxed, high, low, lateral, central, carry, given, sems,
):
    info = facts(info)
    fetched = [pltpu.make_async_copy(initial.at[:, x], adjoint.at[:, x], sems.at[x]) for x in range(EX)]
    for x in range(3):
        fetched[x].start()
    stencil_setup(high, low)

    zero = jnp.zeros((BLOCK, BLOCK), BF16)
    h, l = split(precond[...])
    given[0:BLOCK, :] = jnp.concatenate([h, l], axis=1)
    given[BLOCK:, :] = jnp.concatenate([h, zero], axis=1)
    right = jnp.concatenate([jnp.concatenate([h, l], axis=1)] * 2, axis=0)
    stacked = jnp.concatenate([faces[...].reshape(6 * BLOCK, BLOCK), OMEGA * block_matrix[...], coupling[...]], axis=0)
    h, l = split(folded(both(stacked), right))
    for d in range(4):
        rows = slice(d * BLOCK, (d + 1) * BLOCK)
        lateral[rows, :] = jnp.concatenate([h[rows], l[rows]], axis=1)
        lateral[(d + 4) * BLOCK : (d + 5) * BLOCK, :] = jnp.concatenate([h[rows], zero], axis=1)
    parts = [slice(d * BLOCK, (d + 1) * BLOCK) for d in (6, 4, 5)]
    central[0:BLOCK, :] = jnp.concatenate([h[rows] for rows in parts] + [l[rows] for rows in parts], axis=1)
    central[BLOCK:, :] = jnp.concatenate([h[rows] for rows in parts] + [zero] * 3, axis=1)
    h, l = h[7 * BLOCK :], l[7 * BLOCK :]
    none = jnp.zeros((SPACE, 2 * BLOCK), BF16)
    carry[...] = jnp.concatenate(
        [jnp.concatenate([h, l], axis=1), none, jnp.concatenate([h, zero[:SPACE]], axis=1), none], axis=0
    )

    def enter(x):
        position = lax.broadcasted_iota(jnp.int32, (NTD, LAYER, BLOCK), 1) + x * LAYER
        fetched[x].wait()
        if x + 3 < EX:
            fetched[x + 3].start()
        value = jnp.where(position < info[0], adjoint[:, x], 0.0)
        adjoint[:, x] = value
        stencil_split(x, value, high, low)

    enter(0)
    enter(1)
    for x in layers(INNER):
        enter(x + 1)
        predict(x, field, adjoint, loads, relaxed, high, low, lateral, central, given, conductance, forcing)
    for x in range(INNER[0][0] + INNER[0][1] + 1, EX):
        enter(x)


def first_prediction(info, initial, forcing, conductance, block_matrix, precond, faces, coupling):
    return pl.pallas_call(
        first_kernel,
        out_shape=[VMEM(STACK, F32)] * 4
        + [VMEM(PADDED, BF16)] * 2
        + [VMEM(LATERAL, BF16), VMEM(CENTRAL, BF16), VMEM(SQUARE, BF16), VMEM(SQUARE, BF16)],
        in_specs=[INV, INH] + [INV] * 6,
        out_specs=[INV] * 10,
        scratch_shapes=[pltpu.SemaphoreType.DMA((EX,))],
        compiler_params=params(16),
        cost_estimate=cost(0.01),
        name="first_inner",
    )(info, initial, forcing, conductance, block_matrix, precond, faces, coupling)


def next_kernel(adjoint, loads, relaxed, lateral, central, field, high, low):
    stencil_setup(high, low)
    for x in range(2):
        stencil_split(x, adjoint[:, x], high, low)
    for x in layers(NEXT_INNER):
        stencil_split(x + 1, adjoint[:, x + 1], high, low)
        predict(x, field, adjoint, loads, relaxed, high, low, lateral, central)


def next_prediction(adjoint, loads, relaxed, lateral, central):
    return pl.pallas_call(
        next_kernel,
        out_shape=[VMEM(STACK, F32), VMEM(PADDED, BF16), VMEM(PADDED, BF16)],
        in_specs=[INV] * 5,
        out_specs=[INV] * 3,
        compiler_params=params(16),
        cost_estimate=cost(0.01),
        name="next_inner",
    )(adjoint, loads, relaxed, lateral, central)


def rows_of(stack, t, runs):
    return jnp.concatenate([stack[t, first : first + count].reshape(count * LAYER, BLOCK) for first, count in runs], axis=0)


def chain(info, field, relaxed, carry, runs, trace, done=None):
    keep = jnp.concatenate(
        [
            (lax.broadcasted_iota(jnp.int32, (count * LAYER, BLOCK), 0) + first * LAYER < info[0]).astype(F32)
            for first, count in runs
        ],
        axis=0,
    ) > 0.5
    for t in reversed(range(NTD)):
        value = rows_of(field, t, runs)
        if trace is not None:
            value = value - rows_of(relaxed, t, runs) * folded(both(trace), carry[...])
        trace = jnp.where(keep, value, 0.0)
        at = 0
        for first, count in runs:
            rows = count * LAYER
            field[t, first : first + count] = trace[at : at + rows].reshape(count, LAYER, BLOCK)
            at += rows
        if done is not None:
            done(t)
    return trace


def packed(trace):
    half = trace.shape[0] // 2
    lane = lax.broadcasted_iota(jnp.int32, (half, BLOCK), 1)
    return jnp.where(lane < SPACE, trace[:half], pltpu.roll(trace[half:], SPACE, 1))


def unpacked(value):
    return jnp.concatenate([value, pltpu.roll(value, SPACE, 1)], axis=0)


def trace_shape(runs):
    return VMEM((len(layers(runs)) * LAYER // 2, BLOCK), F32)


def early_chain(info, field, relaxed, carry, runs, trace):
    @pl.when(info[1] == 1)
    def _():
        trace[...] = packed(chain(info, field, relaxed, carry, runs, None))

    @pl.when(info[1] == 0)
    def _():
        trace[...] = jnp.zeros(trace.shape, F32)


def face_matrix(lateral, d):
    top, bottom = pl.multiple_of(d * BLOCK, BLOCK), pl.multiple_of((d + 4) * BLOCK, BLOCK)
    return jnp.concatenate([lateral[pl.ds(top, BLOCK), :], lateral[pl.ds(bottom, BLOCK), :]], axis=0)


def inner_kernel(predicted, info, pred, relaxed, lateral, carry, y_near, y_far, field, trace):
    info = facts(info)
    ((first, count),) = predicted
    for halo, at, has in ((y_near, near(info, 1), 1), (y_far, far(info, 1), info[5])):
        matrix = face_matrix(lateral, 2 + (at > 0).astype(jnp.int32))
        values = jnp.where(has > 0, halo[:, first : first + count].reshape(NTD * count * EZ, BLOCK), 0.0)
        term = folded(both(values), matrix).reshape(NTD, count, EZ, BLOCK)
        area = (slice(None), pl.ds(first, count), pl.ds(at, EZ))
        field[area] = field[area] - relaxed[area] * term
    early_chain(info, field, relaxed, carry, INNER, trace)


def inner_halos(info, field, relaxed, lateral, carry, y_halos, predicted):
    return pl.pallas_call(
        functools.partial(inner_kernel, predicted),
        out_shape=[VMEM(STACK, F32), trace_shape(INNER)],
        in_specs=[INV] + [INV] * 6,
        out_specs=[INV, INV],
        input_output_aliases={1: 0},
        compiler_params=params(8),
        cost_estimate=cost(2),
        name="inner_halos",
    )(info, field, relaxed, lateral, carry, *y_halos)


def outer_kernel(first_sweep, info, *refs):
    info = facts(info)
    predicted = OUTER if first_sweep else NEXT_OUTER
    if first_sweep:
        conductance, given, forcing, *refs = refs
        (_, _, _, _, _, adjoint, lateral, central, carry, x_near, x_far, y_near, y_far,
         field, high, low, loads, relaxed, trace) = refs
    else:
        conductance = given = forcing = None
        (_, _, _, adjoint, lateral, central, carry, x_near, x_far, y_near, y_far, loads, relaxed,
         field, high, low, trace) = refs
    for halo, x, has in ((x_near, near(info, 0), 1), (x_far, far(info, 0), info[4])):
        h, l = split(jnp.where(has > 0, halo[...], 0.0))
        place = jnp.where(x > 0, EX + 1, 0)
        high[place, :, pl.ds(EZ, LAYER)] = h
        low[place, :, pl.ds(EZ, LAYER)] = l
    for halo, y, has in ((y_near, near(info, 1), 1), (y_far, far(info, 1), info[5])):
        place = pl.multiple_of(jnp.where(y > 0, LAYER + EZ, 0), EZ)
        for x in layers(predicted):
            h, l = split(jnp.where(has > 0, halo[:, x], 0.0))
            high[x + 1, :, pl.ds(place, EZ)] = h
            low[x + 1, :, pl.ds(place, EZ)] = l
    for x in layers(predicted):
        predict(x, field, adjoint, loads, relaxed, high, low, lateral, central, given, conductance, forcing)
    early_chain(info, field, relaxed, carry, OUTER, trace)


def outer_prediction(info, field, high, low, adjoint, lateral, central, carry, halos, loads, relaxed, given, conductance, forcing):
    first_sweep = given is not None
    if first_sweep:
        args = [info, conductance, given, forcing, field, high, low, loads, relaxed, adjoint, lateral, central, carry, *halos]
        outs = [VMEM(STACK, F32), VMEM(PADDED, BF16), VMEM(PADDED, BF16), VMEM(STACK, F32), VMEM(STACK, F32)]
        aliases = {k + 4: k for k in range(5)}
    else:
        args = [info, field, high, low, adjoint, lateral, central, carry, *halos, loads, relaxed]
        outs = [VMEM(STACK, F32), VMEM(PADDED, BF16), VMEM(PADDED, BF16)]
        aliases = {k + 1: k for k in range(3)}
    outs = outs + [trace_shape(OUTER)]
    out = pl.pallas_call(
        functools.partial(outer_kernel, first_sweep),
        out_shape=outs,
        in_specs=[INV] + [INV] * (len(args) - 1),
        out_specs=[INV] * len(outs),
        input_output_aliases=aliases,
        compiler_params=params(16),
        cost_estimate=cost(7),
        name="first_outer" if first_sweep else "next_outer",
    )(*args)
    if first_sweep:
        loads, relaxed = out[3:5]
    return out[0], out[-1], loads, relaxed


def late_chain(info, field, relaxed, carry, trace, runs):
    @pl.when(info[1] == 0)
    def _():
        chain(info, field, relaxed, carry, runs, unpacked(trace[...]))


def late_inner_kernel(info, field, relaxed, carry, trace, out):
    info = facts(info)
    late_chain(info, out, relaxed, carry, trace, INNER)


def late_outer_kernel(info, field, relaxed, carry, trace, out, x_near, x_far, y_near, y_far):
    info = facts(info)
    late_chain(info, out, relaxed, carry, trace, OUTER)
    x_near[...] = out[:, near(info, 0)]
    x_far[...] = out[:, far(info, 0)]
    y_near[...] = out[:, :, pl.ds(near(info, 1), EZ)]
    y_far[...] = out[:, :, pl.ds(far(info, 1), EZ)]


def after_trace(info, field, relaxed, carry, trace, inner):
    outs = [VMEM(STACK, F32)] + ([] if inner else FACES)
    return pl.pallas_call(
        late_inner_kernel if inner else late_outer_kernel,
        out_shape=outs,
        in_specs=[INV] + [INV] * 4,
        out_specs=[INV] * len(outs),
        input_output_aliases={1: 0},
        compiler_params=params(8),
        cost_estimate=cost(2),
        name="late_inner" if inner else "late_outer",
    )(info, field, relaxed, carry, trace)


def last_chain(info, relaxed, carry, trace, kept, out, sems, runs):
    copies = [
        [
            pltpu.make_async_copy(kept.at[t, pl.ds(first, count)], out.at[t, pl.ds(first, count)], sems.at[t, k])
            for k, (first, count) in enumerate(runs)
        ]
        for t in range(NTD)
    ]

    def send(t):
        for copy in copies[t]:
            copy.start()

    @pl.when(info[1] == 0)
    def _():
        chain(info, kept, relaxed, carry, runs, unpacked(trace[...]), send)

    @pl.when(info[1] == 1)
    def _():
        for t in range(NTD):
            send(t)

    for t in range(NTD):
        for copy in copies[t]:
            copy.wait()


def last_inner_kernel(info, field, relaxed, carry, trace, kept, out, sems):
    info = facts(info)
    last_chain(info, relaxed, carry, trace, kept, out, sems, INNER)


def last_outer_kernel(info, field, relaxed, carry, trace, given, kept, out, sems):
    info = facts(info)
    last_chain(info, relaxed, carry, trace, kept, out, sems, OUTER)


def last(info, field, relaxed, carry, trace, given):
    inner = given is None
    args = [info, field, relaxed, carry, trace] + ([] if inner else [given])
    return pl.pallas_call(
        last_inner_kernel if inner else last_outer_kernel,
        out_shape=[VMEM(STACK, F32), pltpu.HBM(STACK, F32)],
        in_specs=[INV] + [INV] * 4 + ([] if inner else [INH]),
        out_specs=[INV, INH],
        input_output_aliases={1: 0} if inner else {1: 0, 5: 1},
        scratch_shapes=[pltpu.SemaphoreType.DMA((NTD, 2))],
        compiler_params=params(8),
        cost_estimate=cost(3),
        name="last_inner" if inner else "last_outer",
    )(*args)


def both_ways(pairs):
    return pairs + [(j, i) for i, j in pairs]


def exchanged(value, axis, first):
    count = lax.axis_size(axis)
    return lax.ppermute(value, axis, both_ways([(i, (i + 1) % count) for i in range(first, count, 2)]))


def exchanged_far_x(value):
    count, lines = lax.axis_size("sx"), lax.axis_size("sy")
    pairs = [(i * lines + k, (i + 1) * lines + k) for i in range(1, count - 1, 2) for k in range(lines)]
    pairs += [(i * lines + k, i * lines + k + 1) for i in (0, count - 1) for k in range(0, lines, 2)]
    return lax.ppermute(value, ("sx", "sy"), both_ways(pairs))


def sent_back(value):
    return lax.ppermute(value, "tm", [(1, 0), (0, 1)])


def body(forcing, initial, conductance, counts, block_matrix, precond, face_coupling, time_coupling):
    shape = forcing.shape
    in_hbm = functools.partial(pltpu.with_memory_space_constraint, memory_space=pltpu.HBM)
    forcing, initial = forcing.reshape(STACK), in_hbm(initial.reshape(STACK))
    info = jnp.full((8, BLOCK), counts[0, 0])

    def halos_of(x_near, x_far, y_near, y_far):
        x_far = exchanged_far_x(x_far)
        y_near, y_far = exchanged(y_near, "sy", 0), exchanged(y_far, "sy", 1)
        return exchanged(x_near, "sx", 0), x_far, y_near, y_far

    halos = halos_of(*faces_of_initial(info, initial))
    field, adjoint, loads, relaxed, high, low, lateral, central, carry, given = first_prediction(
        info, initial, forcing, conductance, block_matrix, precond, face_coupling, time_coupling
    )
    for sweep in range(SWEEPS):
        if sweep:
            adjoint, given = field, None
            field, high, low = next_prediction(adjoint, loads, relaxed, lateral, central)
        field, inner = inner_halos(
            info, field, relaxed, lateral, carry, halos[2:], NEXT_INNER if sweep else INNER
        )
        inner = sent_back(inner)
        field, outer, loads, relaxed = outer_prediction(
            info, field, high, low, adjoint, lateral, central, carry, halos, loads, relaxed, given, conductance, forcing
        )
        outer = sent_back(outer)
        if sweep < SWEEPS - 1:
            (field,) = after_trace(info, field, relaxed, carry, inner, True)
            field, *faces = after_trace(info, field, relaxed, carry, outer, False)
            halos = halos_of(*faces)
        else:
            field, out = last(info, field, relaxed, carry, inner, None)
            field, out = last(info, field, relaxed, carry, outer, out)
    return out.reshape(shape)


def solution(mesh):
    in_specs = (
        P("tm", "sx", "sy", None, None),
        P("tm", "sx", "sy", None, None),
        P("tm", "sx", "sy", None),
        P("sx", "sy"),
        P(),
        P(),
        P(),
        P(),
    )
    out_specs = P("tm", "sx", "sy", None, None)
    return jax.shard_map(body, mesh=mesh, in_specs=in_specs, out_specs=out_specs, check_vma=False)
```
